32 devices in a mesh: dp: 2 (over x), ctx: 4 (over y, core), head: 4 (over z).
Axes of the slice: x: 2, y: 2, z: 4, core: 2. Of those that a mesh axis runs over, the one named last changes fastest.
Arguments:
- tokens: bfloat16 [2, 1024, 2048], P('dp', 'ctx'), may hold values from -6 to 6
- proj_weights: bfloat16 [3, 2048, 1024], P(None, None, 'head'), may hold values from -0.125 to 0.125
- init_weight: float32 [8, 128, 128], P('head'), may hold values from -0.5 to 0.5
- base_rates: float32 [8], P('head'), may hold values from 0.005 to 1
- gate_values: float32 [2, 8, 1024], P('dp', 'head', 'ctx'), may hold values from 0.3 to 480
- out_gain: float32 [8, 128], P('head'), may hold values from 0.5 to 1.5
- cotangent: bfloat16 [2, 1024, 1024], P('dp', 'ctx', 'head'), may hold values from -6 to 6
Outputs:
- grad_tokens: bfloat16 [2, 1024, 2048], P('dp', 'ctx', 'head')
- grad_proj: float32 [3, 2048, 1024], P(None, None, 'head')
- grad_init: float32 [8, 128, 128], P('head')
- grad_gain: float32 [8, 128], P('head')
- grad_rates: float32 [8], P('head')
- grad_gates: float32 [2, 8, 1024], P('dp', 'head', 'ctx')
The draws below stay inside these ranges and needn't reach their ends.
All inputs are finite; a program needn't handle non-finite values.
Results may differ from the reference program's by a relative error of at most 0.0072.
Values sent between devices are 32-bit elements; how exact they have to be, the bound alone decides.
A program may use at most 64 MiB of HBM per device.

```python
import jax
import jax.numpy as jnp
from jax import lax

D = 2048
HS = 128
MB = 16
HEADS = 8
SEQS = 2
LEN = 1024


def draw_base_rates(key, part):
    uniform_key = jax.random.fold_in(key, 11)
    exponent = jax.random.uniform(uniform_key, (HEADS,), jnp.float32, jnp.log(0.005), jnp.log(1.0))
    return jnp.clip(jnp.exp(exponent), 0.005, 1.0)


def draw_gate_values(key, part):
    base_key = jax.random.fold_in(key, 21)
    start_key = jax.random.fold_in(key, 22)
    level_key = jax.random.fold_in(key, 23)
    baseline = jax.random.uniform(base_key, (SEQS, HEADS, LEN), jnp.float32, 0.5, 1.0)
    starts = jax.random.randint(start_key, (SEQS, HEADS, 2), 0, LEN // MB - 3) * MB
    places = jnp.arange(LEN, dtype=jnp.int32)
    inside = jnp.any((places[None, None, None, :] >= starts[..., None]) & (places[None, None, None, :] < starts[..., None] + 3 * MB), axis=2)
    levels = jax.random.uniform(level_key, (SEQS, HEADS, LEN), jnp.float32, 300.0, 480.0)
    return jnp.where(inside, levels, baseline)


def block_levels(rng, dims, shards, low, top_value):
    loudness = 1.0
    for axis_at, blocks in shards:
        steps = jax.random.uniform(jax.random.fold_in(jax.random.fold_in(rng, 6), axis_at), (blocks,), jnp.float32, low / len(shards), top_value / len(shards))
        loudness = loudness * jnp.repeat(jnp.exp(steps), dims[axis_at] // blocks).reshape((-1,) + (1,) * (len(dims) - 1 - axis_at))
    return loudness


def gaussian(stream_key, dims, scale, reach, cuts=(), held_as=jnp.bfloat16):
    factor_of = block_levels(stream_key, dims, cuts, -0.22, 0.18) if cuts else 1.0
    result = jax.random.normal(stream_key, dims, jnp.float32) * scale * factor_of
    return jnp.minimum(jnp.maximum(result, -reach), reach).astype(held_as)


def setup_inputs(seed: int = 0) -> dict:
    seeds = jax.random.split(jax.random.key(seed), 8)
    return {
        "tokens": gaussian(seeds[0], (SEQS, LEN, D), 1.0, 6.0, ((0, 2), (1, 4))),
        "proj_weights": gaussian(seeds[1], (3, D, HEADS * HS), D ** -0.5, 0.125, ((2, 4),)),
        "init_weight": gaussian(seeds[2], (HEADS, HS, HS), HS ** -0.5, 0.5, ((0, 4),), jnp.float32),
        "base_rates": draw_base_rates(jax.random.fold_in(seeds[7], 71), 0),
        "gate_values": draw_gate_values(jax.random.fold_in(seeds[7], 71), 0),
        "out_gain": jnp.clip(1.0 + 0.1 * jax.random.normal(seeds[5], (HEADS, HS), jnp.float32), 0.5, 1.5),
        "cotangent": gaussian(seeds[6], (SEQS, LEN, HEADS * HS), 1.0, 6.0, ((0, 2), (1, 4), (2, 4))),
    }


EXACT_MODE = lax.Precision.HIGHEST

def matmul_hi(left, right):
    return jnp.matmul(left, right, precision=EXACT_MODE)

def one_head(query_rows, key_rows, value_rows, first_weight, rate_value, gate_row, gain_row):
    norm_inv = lax.rsqrt(lax.optimization_barrier(jnp.sum(key_rows * key_rows, -1, keepdims=True)) + 1e-06)
    keys = key_rows * norm_inv
    boosted = rate_value * gate_row
    step_rate = boosted / (1.0 + boosted)
    block_count = query_rows.shape[0] // MB
    query_blocks = query_rows.reshape(block_count, MB, HS)
    key_blocks = keys.reshape(block_count, MB, HS)
    value_blocks = value_rows.reshape(block_count, MB, HS)
    rate_blocks = step_rate.reshape(block_count, MB)
    causal = jnp.tril(jnp.ones((MB, MB), jnp.float32))

    def advance(weight, pieces):
        query_block, key_block, value_block, rate_block = pieces
        mixing = matmul_hi(query_block, key_block.T) * causal * rate_block[None, :]
        residual = value_block - matmul_hi(key_block, weight)
        inner_out = matmul_hi(query_block, weight) + matmul_hi(mixing, residual)
        weight = weight + matmul_hi(key_block.T, rate_block[:, None] * residual)
        return (weight, inner_out)
    _, outputs = lax.scan(advance, first_weight, (query_blocks, key_blocks, value_blocks, rate_blocks))
    inner_out = outputs.reshape(-1, HS)
    centred = inner_out - lax.optimization_barrier(jnp.mean(inner_out, -1, keepdims=True))
    normed = centred * lax.rsqrt(lax.optimization_barrier(jnp.mean(centred * centred, -1, keepdims=True)) + 1e-05)
    return query_rows + gain_row * normed

def reference(tokens, proj_weights, init_weight, base_rates, gate_values, out_gain, cotangent):
    flattened = tokens.reshape(-1, D)
    projected = [jnp.dot(flattened, proj_weights[which], preferred_element_type=jnp.float32).astype(jnp.bfloat16) for which in range(3)]

    def heads_first(array):
        return array.reshape(SEQS, LEN, HEADS, HS).transpose(2, 0, 1, 3)

    def per_head(pieces):
        query_all, key_all, value_all, first_weight, rate_value, gate_rows, gain_row, upstream = pieces

        def forward(query_f, key_f, value_f, weight_f, rate_f, gate_f, gain_f):
            return jax.vmap(one_head, in_axes=(0, 0, 0, None, None, 0, None))(query_f, key_f, value_f, weight_f, rate_f, gate_f, gain_f)
        _, pullback = jax.vjp(forward, query_all.astype(jnp.float32), key_all.astype(jnp.float32), value_all.astype(jnp.float32), first_weight, rate_value, gate_rows, gain_row)
        return pullback(upstream.astype(jnp.float32))
    grads = lax.map(per_head, (heads_first(projected[0]), heads_first(projected[1]), heads_first(projected[2]), init_weight, base_rates, gate_values.transpose(1, 0, 2), out_gain, heads_first(cotangent)))
    grad_query, grad_keyraw, grad_value, grad_first, grad_rate, grad_gatev, grad_gainv = grads

    def back_rows(array):
        return array.transpose(1, 2, 0, 3).reshape(SEQS * LEN, HEADS * HS).astype(jnp.bfloat16)
    local_grads = [back_rows(grad_query), back_rows(grad_keyraw), back_rows(grad_value)]
    grad_proj = jnp.stack([lax.dot_general(flattened, local_grads[which], (((0,), (0,)), ((), ())), preferred_element_type=jnp.float32) for which in range(3)])
    token_sum = jnp.dot(local_grads[0], proj_weights[0].T, preferred_element_type=jnp.float32)
    token_sum = token_sum + jnp.dot(local_grads[1], proj_weights[1].T, preferred_element_type=jnp.float32)
    token_sum = token_sum + jnp.dot(local_grads[2], proj_weights[2].T, preferred_element_type=jnp.float32)
    grad_tokens = token_sum.astype(jnp.bfloat16).reshape(SEQS, LEN, D)
    return (grad_tokens, grad_proj, grad_first, grad_gainv, grad_rate, grad_gatev.transpose(1, 0, 2))
```

```python
import functools

import jax
import jax.numpy as jnp
from jax import lax
from jax.experimental import pallas as pl
from jax.experimental.pallas import tpu as pltpu
from jax.sharding import PartitionSpec as P

MB = 16
F32 = jnp.float32
BF16 = jnp.bfloat16
MESH = pl.DeviceIdType.MESH


def split(x):
    if x.dtype == BF16:
        return (x, None)
    high = x.astype(BF16)
    return (high, (x - high.astype(F32)).astype(BF16))


def dot(left, right, dims=(1, 0)):
    def one(a, b):
        return lax.dot_general(a, b, (((dims[0],), (dims[1],)), ((), ())), preferred_element_type=F32)

    total = one(left[0], right[0])
    if right[1] is not None:
        total = total + one(left[0], right[1])
    if left[1] is not None:
        total = total + one(left[1], right[0])
    return total


def pair(parts):
    return tuple(jnp.concatenate(p, axis=1) for p in zip(*parts))


def grid_index(count):
    rows = lax.broadcasted_iota(jnp.int32, (count, count), 0)
    columns = lax.broadcasted_iota(jnp.int32, (count, count), 1)
    return rows, columns


def to_column(row, rows, columns):
    return jnp.sum(jnp.where(rows == columns, row, 0.0), axis=1, keepdims=True)


def to_row(column, rows, columns):
    return jnp.sum(jnp.where(rows == columns, column, 0.0), axis=0, keepdims=True)


def prepare(queries, raw_keys, values, base, gate_row):
    count = queries.shape[0]
    rows, columns = grid_index(count)
    raw = raw_keys.astype(F32)
    norm_inv = lax.rsqrt(jnp.sum(raw * raw, axis=1, keepdims=True) + 1e-06)
    keys = raw * norm_inv
    boost_row = base * gate_row
    rate_row = boost_row / (1.0 + boost_row)
    rate = to_column(rate_row, rows, columns)
    keys_s = split(keys)
    gram = dot(keys_s, keys_s, (1, 1))
    row_block, column_block = rows // MB, columns // MB
    lower = gram * rate_row
    near = (row_block // 2 == column_block // 2) & (row_block > column_block)
    inverse = jnp.where(rows == columns, 1.0, 0.0) - jnp.where(near, lower, 0.0)
    size = 2
    while size * MB < count:
        here = (
            (row_block // (2 * size) == column_block // (2 * size))
            & (row_block // size > column_block // size)
        )
        inverse_s = split(inverse)
        middle = split(dot(inverse_s, split(jnp.where(here, lower, 0.0))))
        inverse = inverse - dot(middle, inverse_s)
        size *= 2
    inverse_s = split(inverse)
    solved = dot(inverse_s, (jnp.concatenate([values, keys_s[0]], 1), jnp.concatenate([jnp.zeros_like(values), keys_s[1]], 1)))
    solved_s = split(solved)
    rate_keys_s = split(rate * keys)
    ends = dot(rate_keys_s, solved_s, (0, 0))
    return dict(
        norm_inv=norm_inv, keys=keys, keys_s=keys_s, boost_row=boost_row, rate=rate, rate_row=rate_row,
        inverse_s=inverse_s, solved=solved, solved_s=solved_s, ends=ends, rate_keys_s=rate_keys_s,
    )


def reach_out(queries, state):
    count, width = queries.shape
    rows, columns = grid_index(count)
    scores = jnp.where(rows >= columns, dot((queries, None), state["keys_s"], (1, 1)), 0.0)
    mixed = dot(split(scores * state["rate_row"]), state["solved_s"])
    state["scores_s"] = split(scores)
    state["reach_s"] = split(queries.astype(F32) - mixed[:, width:])
    state["own_out"] = mixed[:, :width]
    state["pull_s"] = split(dot(state["inverse_s"], state["rate_keys_s"], (0, 0)))


def forward(start, gain, upstream, state):
    width = start.shape[0]
    start_s = split(start)
    inner_out = state["own_out"] + dot(state["reach_s"], start_s)
    solved_keys = (state["solved_s"][0][:, width:], state["solved_s"][1][:, width:])
    state["residual"] = state["solved"][:, :width] - dot(solved_keys, start_s)
    centred = inner_out - jnp.mean(inner_out, axis=1, keepdims=True)
    inv_std = lax.rsqrt(jnp.mean(centred * centred, axis=1, keepdims=True) + 1e-05)
    normed = centred * inv_std
    weighted = upstream * gain
    d_out = inv_std * (
        weighted
        - jnp.mean(weighted, axis=1, keepdims=True)
        - normed * jnp.mean(weighted * normed, axis=1, keepdims=True)
    )
    state["start_s"] = start_s
    state["d_out_s"] = split(d_out)
    state["d_gain"] = jnp.sum(upstream * normed, axis=0, keepdims=True)
    return dot(state["reach_s"], state["d_out_s"], (0, 0))


def query_grad(queries, upstream, state):
    rows, columns = grid_index(queries.shape[0])
    state["rate_res_s"] = split(state["rate"] * state["residual"])
    d_scores = jnp.where(rows >= columns, dot(state["d_out_s"], state["rate_res_s"], (1, 1)), 0.0)
    d_scores_s = split(d_scores)
    d_queries = upstream + dot(state["d_out_s"], state["start_s"], (1, 1)) + dot(d_scores_s, state["keys_s"])
    state["d_scores_s"] = d_scores_s
    return d_queries


def before_end(queries, state):
    state["from_scores"] = dot(state["d_scores_s"], (queries, None), (0, 0))
    pushed = state["rate"] * dot(state["scores_s"], state["d_out_s"], (0, 0))
    state["d_val"] = dot(state["inverse_s"], split(pushed), (0, 0))


def key_value_grad(end_grad, base, gate_row, state):
    rows, columns = grid_index(state["keys"].shape[0])
    end_s = split(end_grad)
    d_val = state["d_val"] + dot(state["pull_s"], end_s)
    d_val_s = split(d_val)
    strict = rows // MB > columns // MB
    d_lower = jnp.where(strict, dot(d_val_s, state["rate_res_s"], (1, 1)), 0.0)
    d_gram_s = split(d_lower + d_lower.T)
    d_keys = (
        state["from_scores"]
        - dot(d_val_s, state["start_s"], (1, 1))
        + dot(state["rate_res_s"], end_s, (1, 1))
        - dot(d_gram_s, state["keys_s"])
    )
    keys = state["keys"]
    d_raw = state["norm_inv"] * (d_keys - keys * jnp.sum(keys * d_keys, axis=1, keepdims=True))
    d_rate = jnp.sum(state["residual"] * d_val, axis=1, keepdims=True) / state["rate"]
    boost = state["boost_row"]
    d_boost = to_row(d_rate, rows, columns) / ((1.0 + boost) * (1.0 + boost))
    return d_raw, d_val, d_boost * base, jnp.sum(d_boost * gate_row, axis=1, keepdims=True)


def kernel(
    sizes,
    tok_ref, w_ref, init_ref, rates_ref, gate_ref, gain_ref, cot_ref,
    gt_out, proj_out, ext_out, gates_out,
    tok_t, maps, maps_all, pulls, pulls_all, acc, ext, full, ext_full, landing, ext_landing, part, part_in,
    maps_send, maps_recv, pulls_send, pulls_recv, part_send, part_recv, red_send, red_recv, done_sem,
):
    n_dp, n_ctx, n_head = sizes
    count, model = tok_ref.shape
    heads, width, _ = init_ref.shape
    dp, ctx, head = lax.axis_index("dp"), lax.axis_index("ctx"), lax.axis_index("head")
    place = {"dp": dp, "ctx": ctx}

    def flip(axis, bit):
        step = 1 << bit
        mine = lax.rem(place[axis] // step, 2)
        return mine, place[axis] + step - 2 * step * mine

    dp_bits = [("dp", b) for b in range(n_dp.bit_length() - 1)]
    ctx_bits = [("ctx", b) for b in range(n_ctx.bit_length() - 1)]
    orders = (ctx_bits + dp_bits, ctx_bits[:1] + dp_bits + ctx_bits[1:])
    stages = len(orders[0])

    barrier = pltpu.get_barrier_semaphore()
    for off in range(1, n_ctx):
        pl.semaphore_signal(barrier, inc=1, device_id={"ctx": lax.rem(ctx + off, n_ctx)}, device_id_type=MESH)
    for off in range(1, n_head):
        pl.semaphore_signal(barrier, inc=1, device_id={"head": lax.rem(head + off, n_head)}, device_id_type=MESH)
    for axis, bit in dp_bits:
        pl.semaphore_signal(barrier, inc=1, device_id={axis: flip(axis, bit)[1]}, device_id_type=MESH)

    tokens = tok_ref[...]
    projected = [
        jnp.dot(tokens, w_ref[which], preferred_element_type=F32).astype(BF16) for which in range(3)
    ]
    span = [slice(h * width, (h + 1) * width) for h in range(heads)]
    queries = [projected[0][:, s] for s in span]
    states = []
    rows, columns = grid_index(width)
    eye = jnp.where(rows == columns, 1.0, 0.0)
    for h in range(heads):
        state = prepare(
            queries[h], projected[1][:, span[h]], projected[2][:, span[h]], rates_ref[h], gate_ref[0, h : h + 1, :]
        )
        states.append(state)
        maps[h, 0] = eye - state["ends"][:, width:]
        maps[h, 1] = state["ends"][:, :width]

    pl.semaphore_wait(barrier, (n_ctx - 1) + (n_head - 1) + len(dp_bits))

    def share(block, slots, send, recv):
        slots[pl.ds(ctx, 1)] = block[...][None]
        copies = []
        for off in range(1, n_ctx):
            copy = pltpu.make_async_remote_copy(
                src_ref=block, dst_ref=slots.at[ctx], send_sem=send.at[off - 1], recv_sem=recv.at[off - 1],
                device_id={"ctx": lax.rem(ctx + off, n_ctx)}, device_id_type=MESH,
            )
            copy.start()
            copies.append(copy)
        return copies

    copies = share(maps, maps_all, maps_send, maps_recv)
    for h in range(heads):
        reach_out(queries[h], states[h])
    tok_t[...] = tokens.T
    for copy in copies:
        copy.wait()

    upstreams = []
    for h in range(heads):
        start = init_ref[h]
        for i in range(n_ctx - 1):
            moved = dot(split(maps_all[i, h, 0]), split(start)) + maps_all[i, h, 1]
            start = jnp.where(ctx > i, moved, start)
        upstream = cot_ref[:, span[h]].astype(F32)
        upstreams.append(upstream)
        pulls[h] = forward(start, gain_ref[h : h + 1, :], upstream, states[h])
    copies = share(pulls, pulls_all, pulls_send, pulls_recv)

    half = model // 2
    work = [(which * 2 + part_, acc, full, landing, (which * 2 + part_) * half, half, orders[part_]) for which in range(3) for part_ in range(2)]
    work.append((6, ext, ext_full, ext_landing, 0, ext.shape[0], orders[0]))
    at = {item[0]: item[4] for item in work}
    flight = {}

    def reduce_start(item, stage):
        number, source, _, land, base, length, order = item
        axis, bit = order[stage]
        mine, partner = flip(axis, bit)
        length = length >> (stage + 1)
        slot = (0 if number == 6 else number * half) + (item[5] - (item[5] >> stage))
        away = pl.multiple_of(at[number] + (1 - mine) * length, 8)
        copy = pltpu.make_async_remote_copy(
            src_ref=source.at[pl.ds(away, length)], dst_ref=land.at[pl.ds(slot, length)],
            send_sem=red_send.at[number, stage], recv_sem=red_recv.at[number, stage],
            device_id={axis: partner}, device_id_type=MESH,
        )
        copy.start()
        flight[number] = (copy, slot, length)
        at[number] = pl.multiple_of(at[number] + mine * length, 8)

    def reduce_end(item, stage):
        number, source, target, land = item[:4]
        copy, slot, length = flight[number]
        copy.wait()
        total = source[pl.ds(at[number], length)] + land[pl.ds(slot, length)]
        (target if stage == stages - 1 else source)[pl.ds(at[number], length)] = total

    def gather_start(item, stage):
        number, _, target, _, _, length, order = item
        axis, bit = order[stage]
        mine, partner = flip(axis, bit)
        length = length >> (stage + 1)
        window = target.at[pl.ds(at[number], length)]
        copy = pltpu.make_async_remote_copy(
            src_ref=window, dst_ref=window,
            send_sem=red_send.at[number, 2 * stages - 1 - stage], recv_sem=red_recv.at[number, 2 * stages - 1 - stage],
            device_id={axis: partner}, device_id_type=MESH,
        )
        copy.start()
        flight[number] = (copy, None, None)
        at[number] = pl.multiple_of(at[number] - mine * length, 8)

    def project(which, grads):
        grad = jnp.concatenate(grads, axis=1).astype(BF16)
        for part_ in range(2):
            where = pl.ds((which * 2 + part_) * half, half)
            acc[where] = jnp.dot(tok_t[pl.ds(part_ * half, half)], grad, preferred_element_type=F32)
            reduce_start(work[which * 2 + part_], 0)
        return grad

    d_rows = [None] * 3
    d_rows[0] = project(0, [query_grad(queries[h], upstreams[h], states[h]) for h in range(heads)])
    for h in range(heads):
        before_end(queries[h], states[h])
    for copy in copies:
        copy.wait()

    results = []
    ext[...] = jnp.zeros_like(ext)
    for h in range(heads):
        grad = jnp.zeros((width, width), F32)
        end_grad = grad
        for i in reversed(range(n_ctx)):
            end_grad = jnp.where(ctx == i, grad, end_grad)
            grad = dot(split(maps_all[i, h, 0]), split(grad), (0, 0)) + pulls_all[i, h]
        ext[0:width, span[h]] = jnp.where(ctx == 0, grad, 0.0)
        d_raw, d_val, gates, d_base = key_value_grad(end_grad, rates_ref[h], gate_ref[0, h : h + 1, :], states[h])
        results.append((d_raw, d_val))
        gates_out[0, h : h + 1, :] = gates
        ext[width : width + 1, span[h]] = states[h]["d_gain"]
        ext[width + 8 : width + 9, span[h]] = jnp.broadcast_to(d_base, (1, width))
    d_rows[1] = project(1, [r[0] for r in results])
    d_rows[2] = project(2, [r[1] for r in results])
    reduce_start(work[6], 0)

    share_ = model // n_head

    def token_part(which_head):
        total = None
        for which in range(3):
            weight = w_ref[which, pl.ds(pl.multiple_of(which_head * share_, share_), share_), :]
            term = lax.dot_general(d_rows[which], weight, (((1,), (1,)), ((), ())), preferred_element_type=F32)
            total = term if total is None else total + term
        return total

    part_copies = []
    for off in range(1, n_head):
        to = lax.rem(head + off, n_head)
        part[off - 1] = token_part(to)
        copy = pltpu.make_async_remote_copy(
            src_ref=part.at[off - 1], dst_ref=part_in.at[off - 1],
            send_sem=part_send.at[off - 1], recv_sem=part_recv.at[off - 1],
            device_id={"head": to}, device_id_type=MESH,
        )
        copy.start()
        part_copies.append(copy)
    own_part = token_part(head)

    for stage in range(stages):
        for item in work:
            reduce_end(item, stage)
            if stage + 1 < stages:
                reduce_start(item, stage + 1)
            else:
                gather_start(item, stage)
    for stage in reversed(range(stages - 1)):
        for item in work:
            flight[item[0]][0].wait()
            gather_start(item, stage)
    for copy in part_copies:
        copy.wait()
    for off in range(1, n_head):
        own_part = own_part + part_in[off - 1]
    gt_out[...] = own_part.astype(BF16)
    outs = []
    for item in work:
        number, _, target, _, base, length, _ = item
        flight[number][0].wait()
        if number < 6:
            copy = pltpu.make_async_copy(target.at[pl.ds(base, length)], proj_out.at[pl.ds(base, length)], done_sem.at[number])
            copy.start()
            outs.append(copy)
        else:
            ext_out[...] = ext_full[...]
    for copy in outs:
        copy.wait()


def body(sizes, tokens, proj_weights, init_weight, base_rates, gate_values, out_gain, cotangent):
    flattened = tokens.reshape(-1, tokens.shape[-1])
    count, model = flattened.shape
    heads, width, _ = init_weight.shape
    n_dp, n_ctx, n_head = sizes
    stages = (n_dp * n_ctx).bit_length() - 1
    span = heads * width
    ext_rows = 256
    vmem, dma = pltpu.VMEM, pltpu.SemaphoreType.DMA
    in_vmem = pl.BlockSpec(memory_space=vmem)
    tokens_grad, proj, ext, gates = pl.pallas_call(
        functools.partial(kernel, sizes),
        out_shape=(
            jax.ShapeDtypeStruct((count, model // n_head), BF16),
            jax.ShapeDtypeStruct((3 * model, span), F32),
            jax.ShapeDtypeStruct((ext_rows, span), F32),
            jax.ShapeDtypeStruct(gate_values.shape, F32),
        ),
        in_specs=[in_vmem] * 3 + [pl.BlockSpec(memory_space=pltpu.SMEM)] + [in_vmem] * 3,
        out_specs=(in_vmem, pl.BlockSpec(memory_space=pl.ANY), in_vmem, in_vmem),
        scratch_shapes=[
            vmem((model, count), BF16),
            vmem((heads, 2, width, width), F32),
            vmem((n_ctx, heads, 2, width, width), F32),
            vmem((heads, width, width), F32),
            vmem((n_ctx, heads, width, width), F32),
            vmem((3 * model, span), F32),
            vmem((ext_rows, span), F32),
            vmem((3 * model, span), F32),
            vmem((ext_rows, span), F32),
            vmem((3 * model, span), F32),
            vmem((ext_rows, span), F32),
            vmem((n_head - 1, count, model // n_head), F32),
            vmem((n_head - 1, count, model // n_head), F32),
            dma((n_ctx - 1,)), dma((n_ctx - 1,)), dma((n_ctx - 1,)), dma((n_ctx - 1,)),
            dma((n_head - 1,)), dma((n_head - 1,)),
            dma((7, 2 * stages)), dma((7, 2 * stages)), dma((6,)),
        ],
        compiler_params=pltpu.CompilerParams(
            collective_id=0, has_side_effects=True, vmem_limit_bytes=56 * 1024 * 1024
        ),
        cost_estimate=pl.CostEstimate(flops=4_000_000_000, bytes_accessed=12_000_000, transcendentals=0),
    )(
        flattened, proj_weights, init_weight, base_rates, gate_values, out_gain,
        cotangent.reshape(count, span),
    )
    grad_init = jnp.stack([ext[:width, h * width : (h + 1) * width] for h in range(heads)])
    grad_gain = ext[width].reshape(heads, width)
    grad_rates = ext[width + 8].reshape(heads, width)[:, 0]
    return (
        tokens_grad[None], proj.reshape(3, model, span), grad_init, grad_gain, grad_rates, gates,
    )


def solution(mesh):
    sizes = (mesh.shape["dp"], mesh.shape["ctx"], mesh.shape["head"])
    in_specs = (
        P("dp", "ctx", None),
        P(None, None, "head"),
        P("head", None, None),
        P("head"),
        P("dp", "head", "ctx"),
        P("head", None),
        P("dp", "ctx", "head"),
    )
    out_specs = (
        P("dp", "ctx", "head"),
        P(None, None, "head"),
        P("head", None, None),
        P("head", None),
        P("head"),
        P("dp", "head", "ctx"),
    )
    return jax.shard_map(
        functools.partial(body, sizes), mesh=mesh, in_specs=in_specs, out_specs=out_specs, check_vma=False
    )
```

```python
import functools

import jax
import jax.numpy as jnp
from jax import lax
from jax.experimental import pallas as pl
from jax.experimental.pallas import tpu as pltpu
from jax.sharding import PartitionSpec as P

MB = 16
F32 = jnp.float32
BF16 = jnp.bfloat16
MESH = pl.DeviceIdType.MESH


def split(x):
    if x.dtype == BF16:
        return (x, None)
    high = x.astype(BF16)
    return (high, (x - high.astype(F32)).astype(BF16))


def dot(left, right, dims=(1, 0)):
    def one(a, b):
        return lax.dot_general(a, b, (((dims[0],), (dims[1],)), ((), ())), preferred_element_type=F32)

    total = one(left[0], right[0])
    if right[1] is not None:
        total = total + one(left[0], right[1])
    if left[1] is not None:
        total = total + one(left[1], right[0])
    return total


def together(steps):
    results = [None] * len(steps)
    open_ = list(range(len(steps)))
    while open_:
        for at in list(open_):
            try:
                next(steps[at])
            except StopIteration as end:
                results[at] = end.value
                open_.remove(at)
    return results


def grid_index(count):
    rows = lax.broadcasted_iota(jnp.int32, (count, count), 0)
    columns = lax.broadcasted_iota(jnp.int32, (count, count), 1)
    return rows, columns


def to_column(row, rows, columns):
    return jnp.sum(jnp.where(rows == columns, row, 0.0), axis=1, keepdims=True)


def to_row(column, rows, columns):
    return jnp.sum(jnp.where(rows == columns, column, 0.0), axis=0, keepdims=True)


def prepare(queries, raw_keys, values, base, gate_row):
    count = queries.shape[0]
    rows, columns = grid_index(count)
    raw = raw_keys.astype(F32)
    norm_inv = lax.rsqrt(jnp.sum(raw * raw, axis=1, keepdims=True) + 1e-06)
    keys = raw * norm_inv
    boost_row = base * gate_row
    rate_row = boost_row / (1.0 + boost_row)
    rate = to_column(rate_row, rows, columns)
    keys_s = split(keys)
    gram = dot(keys_s, keys_s, (1, 1))
    yield
    lower = jnp.where(rows // MB > columns // MB, gram * rate_row, 0.0)
    tile = min(count, 128)
    tile_rows, tile_columns = grid_index(tile)
    row_block, column_block = tile_rows // MB, tile_columns // MB
    eye = jnp.where(tile_rows == tile_columns, 1.0, 0.0)
    tiles = count // tile
    lowers = [lower[t * tile : (t + 1) * tile, t * tile : (t + 1) * tile] for t in range(tiles)]
    near = row_block // 2 == column_block // 2
    inverses = [eye - jnp.where(near, low, 0.0) for low in lowers]
    size = 2
    while size * MB < tile:
        here = (
            (row_block // (2 * size) == column_block // (2 * size))
            & (row_block // size > column_block // size)
        )
        inverses_s = [split(inv) for inv in inverses]
        middles = [dot(inv, split(jnp.where(here, low, 0.0))) for inv, low in zip(inverses_s, lowers)]
        yield
        inverses = [inv - dot(split(mid), inv_s) for inv, mid, inv_s in zip(inverses, middles, inverses_s)]
        yield
        size *= 2
    size = tile
    while size < count:
        joined = []
        for t in range(0, len(inverses), 2):
            low = lower[(t + 1) * size : (t + 2) * size, t * size : (t + 1) * size]
            first_s, second_s = split(inverses[t]), split(inverses[t + 1])
            middle = dot(second_s, split(low))
            yield
            corner = -dot(split(middle), first_s)
            yield
            joined.append(jnp.concatenate([
                jnp.concatenate([inverses[t], jnp.zeros((size, size), F32)], 1),
                jnp.concatenate([corner, inverses[t + 1]], 1),
            ], 0))
        inverses = joined
        size *= 2
    inverse_s = split(inverses[0])
    solved = dot(inverse_s, (jnp.concatenate([values, keys_s[0]], 1), jnp.concatenate([jnp.zeros_like(values), keys_s[1]], 1)))
    yield
    solved_s = split(solved)
    rate_keys_s = split(rate * keys)
    ends = dot(rate_keys_s, solved_s, (0, 0))
    return dict(
        norm_inv=norm_inv, keys=keys, keys_s=keys_s, boost_row=boost_row, rate=rate, rate_row=rate_row,
        inverse_s=inverse_s, solved=solved, solved_s=solved_s, ends=ends, rate_keys_s=rate_keys_s,
    )


def reach_out(queries, state):
    count, width = queries.shape
    rows, columns = grid_index(count)
    scores = jnp.where(rows >= columns, dot((queries, None), state["keys_s"], (1, 1)), 0.0)
    yield
    mixed = dot(split(scores * state["rate_row"]), state["solved_s"])
    yield
    state["scores_s"] = split(scores)
    state["reach_s"] = split(queries.astype(F32) - mixed[:, width:])
    state["own_out"] = mixed[:, :width]
    state["pull_s"] = split(dot(state["inverse_s"], state["rate_keys_s"], (0, 0)))


def forward(start, gain, upstream, state):
    width = start.shape[0]
    start_s = split(start)
    inner_out = state["own_out"] + dot(state["reach_s"], start_s)
    yield
    solved_keys = (state["solved_s"][0][:, width:], state["solved_s"][1][:, width:])
    state["residual"] = state["solved"][:, :width] - dot(solved_keys, start_s)
    yield
    centred = inner_out - jnp.mean(inner_out, axis=1, keepdims=True)
    inv_std = lax.rsqrt(jnp.mean(centred * centred, axis=1, keepdims=True) + 1e-05)
    normed = centred * inv_std
    weighted = upstream * gain
    d_out = inv_std * (
        weighted
        - jnp.mean(weighted, axis=1, keepdims=True)
        - normed * jnp.mean(weighted * normed, axis=1, keepdims=True)
    )
    state["start_s"] = start_s
    state["d_out_s"] = split(d_out)
    state["d_gain"] = jnp.sum(upstream * normed, axis=0, keepdims=True)
    return dot(state["reach_s"], state["d_out_s"], (0, 0))


def query_grad(queries, upstream, state):
    rows, columns = grid_index(queries.shape[0])
    state["rate_res_s"] = split(state["rate"] * state["residual"])
    d_scores = jnp.where(rows >= columns, dot(state["d_out_s"], state["rate_res_s"], (1, 1)), 0.0)
    yield
    d_scores_s = split(d_scores)
    d_queries = upstream + dot(state["d_out_s"], state["start_s"], (1, 1)) + dot(d_scores_s, state["keys_s"])
    yield
    state["d_scores_s"] = d_scores_s
    return d_queries


def before_end(queries, state):
    state["from_scores"] = dot(state["d_scores_s"], (queries, None), (0, 0))
    yield
    pushed = state["rate"] * dot(state["scores_s"], state["d_out_s"], (0, 0))
    yield
    state["d_val"] = dot(state["inverse_s"], split(pushed), (0, 0))


def key_value_grad(end_grad, base, gate_row, state):
    rows, columns = grid_index(state["keys"].shape[0])
    end_s = split(end_grad)
    d_val = state["d_val"] + dot(state["pull_s"], end_s)
    yield
    d_val_s = split(d_val)
    strict = rows // MB > columns // MB
    d_lower = jnp.where(strict, dot(d_val_s, state["rate_res_s"], (1, 1)), 0.0)
    yield
    d_gram_s = split(d_lower + d_lower.T)
    d_keys = (
        state["from_scores"]
        - dot(d_val_s, state["start_s"], (1, 1))
        + dot(state["rate_res_s"], end_s, (1, 1))
        - dot(d_gram_s, state["keys_s"])
    )
    yield
    keys = state["keys"]
    d_raw = state["norm_inv"] * (d_keys - keys * jnp.sum(keys * d_keys, axis=1, keepdims=True))
    d_rate = jnp.sum(state["residual"] * d_val, axis=1, keepdims=True) / state["rate"]
    boost = state["boost_row"]
    d_boost = to_row(d_rate, rows, columns) / ((1.0 + boost) * (1.0 + boost))
    return d_raw, d_val, d_boost * base, jnp.sum(d_boost * gate_row, axis=1, keepdims=True)


def kernel(
    sizes,
    tok_ref, w_ref, init_ref, rates_ref, gate_ref, gain_ref, cot_ref,
    gt_out, proj_out, ext_out, gates_out,
    tok_t, maps, maps_all, pulls, pulls_all, acc, ext, landing, ext_landing, part, part_in,
    maps_send, maps_recv, pulls_send, pulls_recv, part_send, part_recv, red_send, red_recv,
):
    n_dp, n_ctx, n_head = sizes
    count, model = tok_ref.shape
    heads, width, _ = init_ref.shape
    dp, ctx, head = lax.axis_index("dp"), lax.axis_index("ctx"), lax.axis_index("head")
    place = {"dp": dp, "ctx": ctx}

    def flip(axis, bit):
        step = 1 << bit
        mine = lax.rem(place[axis] // step, 2)
        return mine, place[axis] + step - 2 * step * mine

    dp_bits = [("dp", b) for b in range(n_dp.bit_length() - 1)]
    ctx_bits = [("ctx", b) for b in range(n_ctx.bit_length() - 1)]
    orders = (ctx_bits + dp_bits, ctx_bits[:1] + dp_bits + ctx_bits[1:])
    stages = len(orders[0])

    barrier = pltpu.get_barrier_semaphore()
    for off in range(1, n_ctx):
        pl.semaphore_signal(barrier, inc=1, device_id={"ctx": lax.rem(ctx + off, n_ctx)}, device_id_type=MESH)
    for off in range(1, n_head):
        pl.semaphore_signal(barrier, inc=1, device_id={"head": lax.rem(head + off, n_head)}, device_id_type=MESH)
    for axis, bit in dp_bits:
        pl.semaphore_signal(barrier, inc=1, device_id={axis: flip(axis, bit)[1]}, device_id_type=MESH)

    tokens = tok_ref[...]
    projected = [
        jnp.dot(tokens, w_ref[which], preferred_element_type=F32).astype(BF16) for which in range(3)
    ]
    span = [slice(h * width, (h + 1) * width) for h in range(heads)]
    queries = [projected[0][:, s] for s in span]
    rows, columns = grid_index(width)
    eye = jnp.where(rows == columns, 1.0, 0.0)
    states = together([
        prepare(
            queries[h], projected[1][:, span[h]], projected[2][:, span[h]], rates_ref[h], gate_ref[0, h : h + 1, :]
        )
        for h in range(heads)
    ])
    for h in range(heads):
        maps[h, 0] = eye - states[h]["ends"][:, width:]
        maps[h, 1] = states[h]["ends"][:, :width]

    pl.semaphore_wait(barrier, (n_ctx - 1) + (n_head - 1) + len(dp_bits))

    def share(block, slots, send, recv):
        slots[pl.ds(ctx, 1)] = block[...][None]
        copies = []
        for off in range(1, n_ctx):
            copy = pltpu.make_async_remote_copy(
                src_ref=block, dst_ref=slots.at[ctx], send_sem=send.at[off - 1], recv_sem=recv.at[off - 1],
                device_id={"ctx": lax.rem(ctx + off, n_ctx)}, device_id_type=MESH,
            )
            copy.start()
            copies.append(copy)
        return copies

    copies = share(maps, maps_all, maps_send, maps_recv)
    together([reach_out(queries[h], states[h]) for h in range(heads)])
    tok_t[...] = tokens.T
    for copy in copies:
        copy.wait()

    starts = [init_ref[h] for h in range(heads)]
    for i in range(n_ctx - 1):
        for h in range(heads):
            moved = dot(split(maps_all[i, h, 0]), split(starts[h])) + maps_all[i, h, 1]
            starts[h] = jnp.where(ctx > i, moved, starts[h])
    upstreams = [cot_ref[:, span[h]].astype(F32) for h in range(heads)]
    pulled = together([
        forward(starts[h], gain_ref[h : h + 1, :], upstreams[h], states[h]) for h in range(heads)
    ])
    for h in range(heads):
        pulls[h] = pulled[h]
    copies = share(pulls, pulls_all, pulls_send, pulls_recv)

    half = model // 2
    work = [(which * 2 + part_, acc, proj_out, landing, (which * 2 + part_) * half, half, orders[part_]) for which in range(3) for part_ in range(2)]
    work.append((6, ext, ext_out, ext_landing, 0, ext.shape[0], orders[0]))
    at = {item[0]: item[4] for item in work}
    flight = {}

    def reduce_start(item, stage):
        number, source, _, land, base, length, order = item
        axis, bit = order[stage]
        mine, partner = flip(axis, bit)
        length = length >> (stage + 1)
        slot = (0 if number == 6 else number * half) + (item[5] - (item[5] >> stage))
        away = pl.multiple_of(at[number] + (1 - mine) * length, 8)
        copy = pltpu.make_async_remote_copy(
            src_ref=source.at[pl.ds(away, length)], dst_ref=land.at[pl.ds(slot, length)],
            send_sem=red_send.at[number, stage], recv_sem=red_recv.at[number, stage],
            device_id={axis: partner}, device_id_type=MESH,
        )
        copy.start()
        flight[number] = (copy, slot, length)
        at[number] = pl.multiple_of(at[number] + mine * length, 8)

    def reduce_end(item, stage):
        number, source, target, land = item[:4]
        copy, slot, length = flight[number]
        copy.wait()
        total = source[pl.ds(at[number], length)] + land[pl.ds(slot, length)]
        (target if stage == stages - 1 else source)[pl.ds(at[number], length)] = total

    def gather_start(item, stage):
        number, _, target, _, _, length, order = item
        axis, bit = order[stage]
        mine, partner = flip(axis, bit)
        length = length >> (stage + 1)
        window = target.at[pl.ds(at[number], length)]
        copy = pltpu.make_async_remote_copy(
            src_ref=window, dst_ref=window,
            send_sem=red_send.at[number, 2 * stages - 1 - stage], recv_sem=red_recv.at[number, 2 * stages - 1 - stage],
            device_id={axis: partner}, device_id_type=MESH,
        )
        copy.start()
        flight[number] = (copy, None, None)
        at[number] = pl.multiple_of(at[number] - mine * length, 8)

    def project(which, grads):
        grad = jnp.concatenate(grads, axis=1).astype(BF16)
        for part_ in range(2):
            where = pl.ds((which * 2 + part_) * half, half)
            acc[where] = jnp.dot(tok_t[pl.ds(part_ * half, half)], grad, preferred_element_type=F32)
            reduce_start(work[which * 2 + part_], 0)
        return grad

    def advance(item, turn):
        if turn < stages:
            reduce_end(item, turn)
        else:
            flight[item[0]][0].wait()
        if turn + 1 < stages:
            reduce_start(item, turn + 1)
        elif turn + 1 < 2 * stages:
            gather_start(item, 2 * stages - 2 - turn)

    share_ = model // n_head
    d_rows = [None] * 3

    def token_part(which_head, which):
        weight = w_ref[which, pl.ds(pl.multiple_of(which_head * share_, share_), share_), :]
        return lax.dot_general(d_rows[which], weight, (((1,), (1,)), ((), ())), preferred_element_type=F32)

    targets = [lax.rem(head + off, n_head) for off in range(1, n_head)]
    d_rows[0] = project(0, together([query_grad(queries[h], upstreams[h], states[h]) for h in range(heads)]))
    together([before_end(queries[h], states[h]) for h in range(heads)])
    for n, to in enumerate(targets):
        part[n] = token_part(to, 0)
    for copy in copies:
        copy.wait()
    for item in work[:2]:
        advance(item, 0)

    grads = [jnp.zeros((width, width), F32)] * heads
    end_grads = list(grads)
    for i in reversed(range(n_ctx)):
        for h in range(heads):
            end_grads[h] = jnp.where(ctx == i, grads[h], end_grads[h])
            grads[h] = dot(split(maps_all[i, h, 0]), split(grads[h]), (0, 0)) + pulls_all[i, h]
    results = together([
        key_value_grad(end_grads[h], rates_ref[h], gate_ref[0, h : h + 1, :], states[h]) for h in range(heads)
    ])
    d_rows[1] = project(1, [r[0] for r in results])
    d_rows[2] = project(2, [r[1] for r in results])
    for item in work[:2]:
        advance(item, 1)

    part_copies = []
    for n, to in enumerate(targets):
        part[n] = part[n] + token_part(to, 1) + token_part(to, 2)
        copy = pltpu.make_async_remote_copy(
            src_ref=part.at[n], dst_ref=part_in.at[n], send_sem=part_send.at[n], recv_sem=part_recv.at[n],
            device_id={"head": to}, device_id_type=MESH,
        )
        copy.start()
        part_copies.append(copy)
    for item in work[2:6]:
        advance(item, 0)

    ext[...] = jnp.zeros_like(ext)
    for h in range(heads):
        ext[0:width, span[h]] = jnp.where(ctx == 0, grads[h], 0.0)
        gates_out[0, h : h + 1, :] = results[h][2]
        ext[width : width + 1, span[h]] = states[h]["d_gain"]
        ext[width + 8 : width + 9, span[h]] = jnp.broadcast_to(results[h][3], (1, width))
    reduce_start(work[6], 0)
    own_part = token_part(head, 0) + token_part(head, 1) + token_part(head, 2)

    last = 2 * stages - 1
    for turn in range(1, last + 1):
        if turn < last:
            for item in work[:2]:
                advance(item, turn + 1)
        for item in work[2:6]:
            advance(item, turn)
        advance(work[6], turn - 1)
        if turn == last - 1:
            for copy in part_copies:
                copy.wait()
            for n in range(n_head - 1):
                own_part = own_part + part_in[n]
            gt_out[...] = own_part.astype(BF16)
    advance(work[6], last)


def finish_kernel(gt_in, proj_in, ext_in, gates_in, gt_out, proj_out, init_out, gain_out, rates_out, gates_out, sem):
    copy = pltpu.make_async_copy(proj_in, proj_out, sem)
    copy.start()
    heads, width, _ = init_out.shape
    gt_out[...] = gt_in[...]
    gates_out[...] = gates_in[...]
    for h in range(heads):
        span = slice(h * width, (h + 1) * width)
        init_out[h] = ext_in[0:width, span]
        gain_out[h : h + 1, :] = ext_in[width : width + 1, span]
        rates_out[h : h + 1, :] = ext_in[width + 8 : width + 9, h * width : h * width + 1]
    copy.wait()


def body(sizes, tokens, proj_weights, init_weight, base_rates, gate_values, out_gain, cotangent):
    flattened = tokens.reshape(-1, tokens.shape[-1])
    count, model = flattened.shape
    heads, width, _ = init_weight.shape
    n_dp, n_ctx, n_head = sizes
    stages = (n_dp * n_ctx).bit_length() - 1
    span = heads * width
    ext_rows = 256
    vmem, dma = pltpu.VMEM, pltpu.SemaphoreType.DMA
    in_vmem = pl.BlockSpec(memory_space=vmem)
    tokens_grad, proj, ext, gates = pl.pallas_call(
        functools.partial(kernel, sizes),
        out_shape=(
            vmem((count, model // n_head), BF16),
            vmem((3 * model, span), F32),
            vmem((ext_rows, span), F32),
            vmem(gate_values.shape, F32),
        ),
        in_specs=[in_vmem] * 3 + [pl.BlockSpec(memory_space=pltpu.SMEM)] + [in_vmem] * 3,
        out_specs=(in_vmem,) * 4,
        scratch_shapes=[
            vmem((model, count), BF16),
            vmem((heads, 2, width, width), F32),
            vmem((n_ctx, heads, 2, width, width), F32),
            vmem((heads, width, width), F32),
            vmem((n_ctx, heads, width, width), F32),
            vmem((3 * model, span), F32),
            vmem((ext_rows, span), F32),
            vmem((3 * model, span), F32),
            vmem((ext_rows, span), F32),
            vmem((n_head - 1, count, model // n_head), F32),
            vmem((n_head - 1, count, model // n_head), F32),
            dma((n_ctx - 1,)), dma((n_ctx - 1,)), dma((n_ctx - 1,)), dma((n_ctx - 1,)),
            dma((n_head - 1,)), dma((n_head - 1,)),
            dma((7, 2 * stages)), dma((7, 2 * stages)),
        ],
        compiler_params=pltpu.CompilerParams(
            collective_id=0, has_side_effects=True, vmem_limit_bytes=44 * 1024 * 1024
        ),
        cost_estimate=pl.CostEstimate(flops=4_000_000_000, bytes_accessed=12_000_000, transcendentals=0),
    )(
        flattened, proj_weights, init_weight, base_rates, gate_values, out_gain,
        cotangent.reshape(count, span),
    )
    anywhere = pl.BlockSpec(memory_space=pl.ANY)
    tokens_grad, proj, grad_init, grad_gain, grad_rates, gates = pl.pallas_call(
        finish_kernel,
        out_shape=(
            jax.ShapeDtypeStruct((count, model // n_head), BF16),
            jax.ShapeDtypeStruct((3 * model, span), F32),
            jax.ShapeDtypeStruct(init_weight.shape, F32),
            jax.ShapeDtypeStruct(out_gain.shape, F32),
            jax.ShapeDtypeStruct((heads, 1), F32),
            jax.ShapeDtypeStruct(gate_values.shape, F32),
        ),
        in_specs=[in_vmem, anywhere, in_vmem, in_vmem],
        out_specs=(in_vmem, anywhere, in_vmem, in_vmem, in_vmem, in_vmem),
        scratch_shapes=[dma],
        cost_estimate=pl.CostEstimate(flops=0, bytes_accessed=8_000_000, transcendentals=0),
    )(tokens_grad, proj, ext, gates)
    return (
        tokens_grad[None], proj.reshape(3, model, span), grad_init, grad_gain, grad_rates[:, 0], gates,
    )


def solution(mesh):
    sizes = (mesh.shape["dp"], mesh.shape["ctx"], mesh.shape["head"])
    in_specs = (
        P("dp", "ctx", None),
        P(None, None, "head"),
        P("head", None, None),
        P("head"),
        P("dp", "head", "ctx"),
        P("head", None),
        P("dp", "ctx", "head"),
    )
    out_specs = (
        P("dp", "ctx", "head"),
        P(None, None, "head"),
        P("head", None, None),
        P("head", None),
        P("head"),
        P("dp", "head", "ctx"),
    )
    return jax.shard_map(
        functools.partial(body, sizes), mesh=mesh, in_specs=in_specs, out_specs=out_specs, check_vma=False
    )
```

```python
import functools

import jax
import jax.numpy as jnp
from jax import lax
from jax.experimental import pallas as pl
from jax.experimental.pallas import tpu as pltpu
from jax.sharding import PartitionSpec as P

MB = 16
F32 = jnp.float32
BF16 = jnp.bfloat16
MESH = pl.DeviceIdType.MESH


def split(x):
    if x.dtype == BF16:
        return (x, None)
    high = x.astype(BF16)
    return (high, (x - high.astype(F32)).astype(BF16))


def flipped(x):
    return tuple(None if piece is None else piece.T for piece in x)


def dot(left, right, dims=(1, 0)):
    if dims[0] == 0:
        return dot(flipped(left), right, (1, dims[1]))
    terms = [(left[0], right[0])]
    if right[1] is not None:
        terms.append((left[0], right[1]))
    if left[1] is not None:
        terms.append((left[1], right[0]))
    a = jnp.concatenate([t[0] for t in terms], axis=1)
    b = jnp.concatenate([t[1] for t in terms], axis=dims[1])
    return lax.dot_general(a, b, (((1,), (dims[1],)), ((), ())), preferred_element_type=F32)


def together(steps):
    results = [None] * len(steps)
    open_ = list(range(len(steps)))
    while open_:
        for at in list(open_):
            try:
                next(steps[at])
            except StopIteration as end:
                results[at] = end.value
                open_.remove(at)
    return results


def grid_index(count):
    rows = lax.broadcasted_iota(jnp.int32, (count, count), 0)
    columns = lax.broadcasted_iota(jnp.int32, (count, count), 1)
    return rows, columns


def to_column(row, rows, columns):
    return jnp.sum(jnp.where(rows == columns, row, 0.0), axis=1, keepdims=True)


def to_row(column, rows, columns):
    return jnp.sum(jnp.where(rows == columns, column, 0.0), axis=0, keepdims=True)


def prepare(queries, raw_keys, values, base, gate_row):
    count = queries.shape[0]
    rows, columns = grid_index(count)
    raw = raw_keys.astype(F32)
    norm_inv = lax.rsqrt(jnp.sum(raw * raw, axis=1, keepdims=True) + 1e-06)
    keys = raw * norm_inv
    boost_row = base * gate_row
    rate_row = boost_row / (1.0 + boost_row)
    rate = to_column(rate_row, rows, columns)
    keys_s = split(keys)
    gram = dot(keys_s, keys_s, (1, 1))
    yield
    lower = jnp.where(rows // MB > columns // MB, gram * rate_row, 0.0)
    tile = min(count, 128)
    tile_rows, tile_columns = grid_index(tile)
    row_block, column_block = tile_rows // MB, tile_columns // MB
    eye = jnp.where(tile_rows == tile_columns, 1.0, 0.0)
    tiles = count // tile
    lowers = [lower[t * tile : (t + 1) * tile, t * tile : (t + 1) * tile] for t in range(tiles)]
    near = row_block // 2 == column_block // 2
    inverses = [eye - jnp.where(near, low, 0.0) for low in lowers]
    size = 2
    while size * MB < tile:
        here = (
            (row_block // (2 * size) == column_block // (2 * size))
            & (row_block // size > column_block // size)
        )
        inverses_s = [split(inv) for inv in inverses]
        middles = [dot(inv, split(jnp.where(here, low, 0.0))) for inv, low in zip(inverses_s, lowers)]
        yield
        inverses = [inv - dot(split(mid), inv_s) for inv, mid, inv_s in zip(inverses, middles, inverses_s)]
        yield
        size *= 2
    size = tile
    while size < count:
        joined = []
        for t in range(0, len(inverses), 2):
            low = lower[(t + 1) * size : (t + 2) * size, t * size : (t + 1) * size]
            first_s, second_s = split(inverses[t]), split(inverses[t + 1])
            middle = dot(second_s, split(low))
            yield
            corner = -dot(split(middle), first_s)
            yield
            joined.append(jnp.concatenate([
                jnp.concatenate([inverses[t], jnp.zeros((size, size), F32)], 1),
                jnp.concatenate([corner, inverses[t + 1]], 1),
            ], 0))
        inverses = joined
        size *= 2
    inverse_s = split(inverses[0])
    solved = dot(inverse_s, (jnp.concatenate([values, keys_s[0]], 1), jnp.concatenate([jnp.zeros_like(values), keys_s[1]], 1)))
    yield
    solved_s = split(solved)
    rate_keys_s = split(rate * keys)
    ends = dot(rate_keys_s, solved_s, (0, 0))
    return dict(
        norm_inv=norm_inv, keys=keys, keys_s=keys_s, boost_row=boost_row, rate=rate, rate_row=rate_row,
        inverse_s=inverse_s, solved=solved, solved_s=solved_s, ends=ends, rate_keys_s=rate_keys_s,
    )


def reach_out(queries, state):
    count, width = queries.shape
    rows, columns = grid_index(count)
    scores = jnp.where(rows >= columns, dot((queries, None), state["keys_s"], (1, 1)), 0.0)
    yield
    mixed = dot(split(scores * state["rate_row"]), state["solved_s"])
    yield
    state["scores_s"] = split(scores)
    state["reach_s"] = split(queries.astype(F32) - mixed[:, width:])
    state["own_out"] = mixed[:, :width]
    state["inverse_t"] = flipped(state["inverse_s"])
    state["pull_s"] = split(dot(state["inverse_t"], state["rate_keys_s"]))


def forward(start, gain, upstream, state):
    width = start.shape[0]
    start_s = split(start)
    inner_out = state["own_out"] + dot(state["reach_s"], start_s)
    yield
    solved_keys = (state["solved_s"][0][:, width:], state["solved_s"][1][:, width:])
    state["residual"] = state["solved"][:, :width] - dot(solved_keys, start_s)
    yield
    centred = inner_out - jnp.mean(inner_out, axis=1, keepdims=True)
    inv_std = lax.rsqrt(jnp.mean(centred * centred, axis=1, keepdims=True) + 1e-05)
    normed = centred * inv_std
    weighted = upstream * gain
    d_out = inv_std * (
        weighted
        - jnp.mean(weighted, axis=1, keepdims=True)
        - normed * jnp.mean(weighted * normed, axis=1, keepdims=True)
    )
    state["start_s"] = start_s
    state["d_out_s"] = split(d_out)
    state["d_gain"] = jnp.sum(upstream * normed, axis=0, keepdims=True)
    return dot(state["reach_s"], state["d_out_s"], (0, 0))


def query_grad(queries, upstream, state):
    rows, columns = grid_index(queries.shape[0])
    state["rate_res_s"] = split(state["rate"] * state["residual"])
    d_scores = jnp.where(rows >= columns, dot(state["d_out_s"], state["rate_res_s"], (1, 1)), 0.0)
    yield
    d_scores_s = split(d_scores)
    d_queries = upstream + dot(state["d_out_s"], state["start_s"], (1, 1)) + dot(d_scores_s, state["keys_s"])
    yield
    state["d_scores_s"] = d_scores_s
    return d_queries


def before_end(queries, state):
    state["from_scores"] = dot(state["d_scores_s"], (queries, None), (0, 0))
    yield
    pushed = state["rate"] * dot(state["scores_s"], state["d_out_s"], (0, 0))
    yield
    state["d_val"] = dot(state["inverse_t"], split(pushed))


def key_value_grad(end_grad, base, gate_row, state):
    rows, columns = grid_index(state["keys"].shape[0])
    end_s = split(end_grad)
    d_val = state["d_val"] + dot(state["pull_s"], end_s)
    yield
    d_val_s = split(d_val)
    strict = rows // MB > columns // MB
    d_lower = jnp.where(strict, dot(d_val_s, state["rate_res_s"], (1, 1)), 0.0)
    yield
    d_gram_s = split(d_lower + d_lower.T)
    d_keys = (
        state["from_scores"]
        - dot(d_val_s, state["start_s"], (1, 1))
        + dot(state["rate_res_s"], end_s, (1, 1))
        - dot(d_gram_s, state["keys_s"])
    )
    yield
    keys = state["keys"]
    d_raw = state["norm_inv"] * (d_keys - keys * jnp.sum(keys * d_keys, axis=1, keepdims=True))
    d_rate = jnp.sum(state["residual"] * d_val, axis=1, keepdims=True) / state["rate"]
    boost = state["boost_row"]
    d_boost = to_row(d_rate, rows, columns) / ((1.0 + boost) * (1.0 + boost))
    return d_raw, d_val, d_boost * base, jnp.sum(d_boost * gate_row, axis=1, keepdims=True)


def kernel(
    sizes,
    tok_ref, w_hbm, init_ref, rates_ref, gate_ref, gain_ref, cot_ref,
    gt_out, proj_out, ext_out, gates_out,
    w_ref, tok_t, maps, maps_all, pulls, pulls_all, acc, ext, landing, ext_landing, part, part_in,
    maps_send, maps_recv, pulls_send, pulls_recv, part_send, part_recv, red_send, red_recv, w_sem,
):
    n_dp, n_ctx, n_head = sizes
    count, model = tok_ref.shape
    heads, width, _ = init_ref.shape
    dp, ctx, head = lax.axis_index("dp"), lax.axis_index("ctx"), lax.axis_index("head")
    place = {"dp": dp, "ctx": ctx}
    w_copies = [pltpu.make_async_copy(w_hbm.at[which], w_ref.at[which], w_sem.at[which]) for which in (1, 2, 0)]
    for copy in w_copies:
        copy.start()

    def flip(axis, bit):
        step = 1 << bit
        mine = lax.rem(place[axis] // step, 2)
        return mine, place[axis] + step - 2 * step * mine

    dp_bits = [("dp", b) for b in range(n_dp.bit_length() - 1)]
    ctx_bits = [("ctx", b) for b in range(n_ctx.bit_length() - 1)]
    orders = (ctx_bits + dp_bits, ctx_bits[:1] + dp_bits + ctx_bits[1:])
    stages = len(orders[0])

    barrier = pltpu.get_barrier_semaphore()
    for off in range(1, n_ctx):
        pl.semaphore_signal(barrier, inc=1, device_id={"ctx": lax.rem(ctx + off, n_ctx)}, device_id_type=MESH)
    for off in range(1, n_head):
        pl.semaphore_signal(barrier, inc=1, device_id={"head": lax.rem(head + off, n_head)}, device_id_type=MESH)
    for axis, bit in dp_bits:
        pl.semaphore_signal(barrier, inc=1, device_id={axis: flip(axis, bit)[1]}, device_id_type=MESH)

    tokens = tok_ref[...]
    projected = [None] * 3
    for which in (1, 2, 0):
        w_copies[(1, 2, 0).index(which)].wait()
        projected[which] = jnp.dot(tokens, w_ref[which], preferred_element_type=F32).astype(BF16)
    span = [slice(h * width, (h + 1) * width) for h in range(heads)]
    queries = [projected[0][:, s] for s in span]
    rows, columns = grid_index(width)
    eye = jnp.where(rows == columns, 1.0, 0.0)
    states = together([
        prepare(
            queries[h], projected[1][:, span[h]], projected[2][:, span[h]], rates_ref[h], gate_ref[0, h : h + 1, :]
        )
        for h in range(heads)
    ])
    for h in range(heads):
        maps[h, 0] = eye - states[h]["ends"][:, width:]
        maps[h, 1] = states[h]["ends"][:, :width]

    pl.semaphore_wait(barrier, (n_ctx - 1) + (n_head - 1) + len(dp_bits))

    def share(block, slots, send, recv):
        slots[pl.ds(ctx, 1)] = block[...][None]
        copies = []
        for off in range(1, n_ctx):
            copy = pltpu.make_async_remote_copy(
                src_ref=block, dst_ref=slots.at[ctx], send_sem=send.at[off - 1], recv_sem=recv.at[off - 1],
                device_id={"ctx": lax.rem(ctx + off, n_ctx)}, device_id_type=MESH,
            )
            copy.start()
            copies.append(copy)
        return copies

    copies = share(maps, maps_all, maps_send, maps_recv)
    together([reach_out(queries[h], states[h]) for h in range(heads)])
    tok_t[...] = tokens.T
    for copy in copies:
        copy.wait()

    starts = [init_ref[h] for h in range(heads)]
    for i in range(n_ctx - 1):
        for h in range(heads):
            moved = dot(split(maps_all[i, h, 0]), split(starts[h])) + maps_all[i, h, 1]
            starts[h] = jnp.where(ctx > i, moved, starts[h])
    upstreams = [cot_ref[:, span[h]].astype(F32) for h in range(heads)]
    pulled = together([
        forward(starts[h], gain_ref[h : h + 1, :], upstreams[h], states[h]) for h in range(heads)
    ])
    for h in range(heads):
        pulls[h] = pulled[h]
    copies = share(pulls, pulls_all, pulls_send, pulls_recv)

    half = model // 2
    work = [(which * 2 + part_, acc, proj_out, landing, (which * 2 + part_) * half, half, orders[part_]) for which in range(3) for part_ in range(2)]
    work.append((6, ext, ext_out, ext_landing, 0, ext.shape[0], orders[0]))
    at = {item[0]: item[4] for item in work}
    flight = {}

    def reduce_start(item, stage):
        number, source, _, land, base, length, order = item
        axis, bit = order[stage]
        mine, partner = flip(axis, bit)
        length = length >> (stage + 1)
        slot = (0 if number == 6 else number * half) + (item[5] - (item[5] >> stage))
        away = pl.multiple_of(at[number] + (1 - mine) * length, 8)
        copy = pltpu.make_async_remote_copy(
            src_ref=source.at[pl.ds(away, length)], dst_ref=land.at[pl.ds(slot, length)],
            send_sem=red_send.at[number, stage], recv_sem=red_recv.at[number, stage],
            device_id={axis: partner}, device_id_type=MESH,
        )
        copy.start()
        flight[number] = (copy, slot, length)
        at[number] = pl.multiple_of(at[number] + mine * length, 8)

    def reduce_end(item, stage):
        number, source, target, land = item[:4]
        copy, slot, length = flight[number]
        copy.wait()
        total = source[pl.ds(at[number], length)] + land[pl.ds(slot, length)]
        (target if stage == stages - 1 else source)[pl.ds(at[number], length)] = total

    def gather_start(item, stage):
        number, _, target, _, _, length, order = item
        axis, bit = order[stage]
        mine, partner = flip(axis, bit)
        length = length >> (stage + 1)
        window = target.at[pl.ds(at[number], length)]
        copy = pltpu.make_async_remote_copy(
            src_ref=window, dst_ref=window,
            send_sem=red_send.at[number, 2 * stages - 1 - stage], recv_sem=red_recv.at[number, 2 * stages - 1 - stage],
            device_id={axis: partner}, device_id_type=MESH,
        )
        copy.start()
        flight[number] = (copy, None, None)
        at[number] = pl.multiple_of(at[number] - mine * length, 8)

    def project(which, grads):
        grad = jnp.concatenate(grads, axis=1).astype(BF16)
        for part_ in range(2):
            where = pl.ds((which * 2 + part_) * half, half)
            acc[where] = jnp.dot(tok_t[pl.ds(part_ * half, half)], grad, preferred_element_type=F32)
            reduce_start(work[which * 2 + part_], 0)
        return grad

    def advance(item, turn):
        if turn < stages:
            reduce_end(item, turn)
        else:
            flight[item[0]][0].wait()
        if turn + 1 < stages:
            reduce_start(item, turn + 1)
        elif turn + 1 < 2 * stages:
            gather_start(item, 2 * stages - 2 - turn)

    share_ = model // n_head
    d_rows = [None] * 3

    def token_part(which_head, which):
        weight = w_ref[which, pl.ds(pl.multiple_of(which_head * share_, share_), share_), :]
        return lax.dot_general(d_rows[which], weight, (((1,), (1,)), ((), ())), preferred_element_type=F32)

    targets = [lax.rem(head + off, n_head) for off in range(1, n_head)]
    d_rows[0] = project(0, together([query_grad(queries[h], upstreams[h], states[h]) for h in range(heads)]))
    together([before_end(queries[h], states[h]) for h in range(heads)])
    for n, to in enumerate(targets):
        part[n] = token_part(to, 0)
    for copy in copies:
        copy.wait()
    for item in work[:2]:
        advance(item, 0)

    grads = [jnp.zeros((width, width), F32)] * heads
    end_grads = list(grads)
    for i in reversed(range(n_ctx)):
        for h in range(heads):
            end_grads[h] = jnp.where(ctx == i, grads[h], end_grads[h])
            grads[h] = dot(split(maps_all[i, h, 0]), split(grads[h]), (0, 0)) + pulls_all[i, h]
    results = together([
        key_value_grad(end_grads[h], rates_ref[h], gate_ref[0, h : h + 1, :], states[h]) for h in range(heads)
    ])
    d_rows[1] = project(1, [r[0] for r in results])
    d_rows[2] = project(2, [r[1] for r in results])
    for item in work[:2]:
        advance(item, 1)

    part_copies = []
    for n, to in enumerate(targets):
        part[n] = part[n] + token_part(to, 1) + token_part(to, 2)
        copy = pltpu.make_async_remote_copy(
            src_ref=part.at[n], dst_ref=part_in.at[n], send_sem=part_send.at[n], recv_sem=part_recv.at[n],
            device_id={"head": to}, device_id_type=MESH,
        )
        copy.start()
        part_copies.append(copy)
    for item in work[2:6]:
        advance(item, 0)

    ext[...] = jnp.zeros_like(ext)
    for h in range(heads):
        ext[0:width, span[h]] = jnp.where(ctx == 0, grads[h], 0.0)
        gates_out[0, h : h + 1, :] = results[h][2]
        ext[width : width + 1, span[h]] = states[h]["d_gain"]
        ext[width + 8 : width + 9, span[h]] = jnp.broadcast_to(results[h][3], (1, width))
    reduce_start(work[6], 0)
    own_part = token_part(head, 0) + token_part(head, 1) + token_part(head, 2)

    last = 2 * stages - 1
    for turn in range(1, last + 1):
        if turn < last:
            for item in work[:2]:
                advance(item, turn + 1)
        for item in work[2:6]:
            advance(item, turn)
        advance(work[6], turn - 1)
        if turn == last - 1:
            for copy in part_copies:
                copy.wait()
            for n in range(n_head - 1):
                own_part = own_part + part_in[n]
            gt_out[...] = own_part.astype(BF16)
    advance(work[6], last)


def finish_kernel(gt_in, proj_in, ext_in, gates_in, gt_out, proj_out, init_out, gain_out, rates_out, gates_out, sem):
    copy = pltpu.make_async_copy(proj_in, proj_out, sem)
    copy.start()
    heads, width, _ = init_out.shape
    gt_out[...] = gt_in[...]
    gates_out[...] = gates_in[...]
    for h in range(heads):
        span = slice(h * width, (h + 1) * width)
        init_out[h] = ext_in[0:width, span]
        gain_out[h : h + 1, :] = ext_in[width : width + 1, span]
        rates_out[h] = jnp.max(ext_in[width + 8 : width + 9, span])
    copy.wait()


def body(sizes, tokens, proj_weights, init_weight, base_rates, gate_values, out_gain, cotangent):
    flattened = tokens.reshape(-1, tokens.shape[-1])
    count, model = flattened.shape
    heads, width, _ = init_weight.shape
    n_dp, n_ctx, n_head = sizes
    stages = (n_dp * n_ctx).bit_length() - 1
    span = heads * width
    ext_rows = 256
    vmem, dma = pltpu.VMEM, pltpu.SemaphoreType.DMA
    in_vmem = pl.BlockSpec(memory_space=vmem)
    tokens_grad, proj, ext, gates = pl.pallas_call(
        functools.partial(kernel, sizes),
        out_shape=(
            vmem((count, model // n_head), BF16),
            vmem((3 * model, span), F32),
            vmem((ext_rows, span), F32),
            vmem(gate_values.shape, F32),
        ),
        in_specs=[in_vmem, pl.BlockSpec(memory_space=pltpu.HBM), in_vmem] + [pl.BlockSpec(memory_space=pltpu.SMEM)] + [in_vmem] * 3,
        out_specs=(in_vmem,) * 4,
        scratch_shapes=[
            vmem(proj_weights.shape, BF16),
            vmem((model, count), BF16),
            vmem((heads, 2, width, width), F32),
            vmem((n_ctx, heads, 2, width, width), F32),
            vmem((heads, width, width), F32),
            vmem((n_ctx, heads, width, width), F32),
            vmem((3 * model, span), F32),
            vmem((ext_rows, span), F32),
            vmem((3 * model, span), F32),
            vmem((ext_rows, span), F32),
            vmem((n_head - 1, count, model // n_head), F32),
            vmem((n_head - 1, count, model // n_head), F32),
            dma((n_ctx - 1,)), dma((n_ctx - 1,)), dma((n_ctx - 1,)), dma((n_ctx - 1,)),
            dma((n_head - 1,)), dma((n_head - 1,)),
            dma((7, 2 * stages)), dma((7, 2 * stages)), dma((3,)),
        ],
        compiler_params=pltpu.CompilerParams(
            collective_id=0, has_side_effects=True, vmem_limit_bytes=44 * 1024 * 1024
        ),
        cost_estimate=pl.CostEstimate(flops=4_000_000_000, bytes_accessed=12_000_000, transcendentals=0),
    )(*(
        pltpu.with_memory_space_constraint(x, pltpu.HBM)
        for x in (
            flattened, proj_weights, init_weight, base_rates, gate_values, out_gain,
            cotangent.reshape(count, span),
        )
    ))
    anywhere = pl.BlockSpec(memory_space=pl.ANY)
    tokens_grad, proj, grad_init, grad_gain, grad_rates, gates = pl.pallas_call(
        finish_kernel,
        out_shape=(
            jax.ShapeDtypeStruct((count, model // n_head), BF16),
            jax.ShapeDtypeStruct((3 * model, span), F32),
            jax.ShapeDtypeStruct(init_weight.shape, F32),
            jax.ShapeDtypeStruct(out_gain.shape, F32),
            jax.ShapeDtypeStruct((heads,), F32),
            jax.ShapeDtypeStruct(gate_values.shape, F32),
        ),
        in_specs=[in_vmem] * 4,
        out_specs=(in_vmem, anywhere, in_vmem, in_vmem, pl.BlockSpec(memory_space=pltpu.SMEM), in_vmem),
        scratch_shapes=[dma],
        compiler_params=pltpu.CompilerParams(vmem_limit_bytes=12 * 1024 * 1024),
        cost_estimate=pl.CostEstimate(flops=0, bytes_accessed=8_000_000, transcendentals=0),
    )(*(pltpu.with_memory_space_constraint(x, pltpu.VMEM) for x in (tokens_grad, proj, ext, gates)))
    return (
        tokens_grad[None], proj.reshape(3, model, span), grad_init, grad_gain, grad_rates, gates,
    )


def solution(mesh):
    sizes = (mesh.shape["dp"], mesh.shape["ctx"], mesh.shape["head"])
    in_specs = (
        P("dp", "ctx", None),
        P(None, None, "head"),
        P("head", None, None),
        P("head"),
        P("dp", "head", "ctx"),
        P("head", None),
        P("dp", "ctx", "head"),
    )
    out_specs = (
        P("dp", "ctx", "head"),
        P(None, None, "head"),
        P("head", None, None),
        P("head", None),
        P("head"),
        P("dp", "head", "ctx"),
    )
    return jax.shard_map(
        functools.partial(body, sizes), mesh=mesh, in_specs=in_specs, out_specs=out_specs, check_vma=False
    )
```

```python
import functools

import jax
import jax.numpy as jnp
from jax import lax
from jax.experimental import pallas as pl
from jax.experimental.pallas import tpu as pltpu
from jax.sharding import PartitionSpec as P

MB = 16
F32 = jnp.float32
BF16 = jnp.bfloat16
MESH = pl.DeviceIdType.MESH


def split(x):
    if x.dtype == BF16:
        return (x, None)
    high = x.astype(BF16)
    return (high, (x - high.astype(F32)).astype(BF16))


def flipped(x):
    return tuple(None if piece is None else piece.T for piece in x)


def dot(left, right, dims=(1, 0)):
    if dims[0] == 0:
        return dot(flipped(left), right, (1, dims[1]))
    terms = [(left[0], right[0])]
    if right[1] is not None:
        terms.append((left[0], right[1]))
    if left[1] is not None:
        terms.append((left[1], right[0]))
    a = jnp.concatenate([t[0] for t in terms], axis=1)
    b = jnp.concatenate([t[1] for t in terms], axis=dims[1])
    return lax.dot_general(a, b, (((1,), (dims[1],)), ((), ())), preferred_element_type=F32)


def together(steps):
    results = [None] * len(steps)
    open_ = list(range(len(steps)))
    while open_:
        for at in list(open_):
            try:
                next(steps[at])
            except StopIteration as end:
                results[at] = end.value
                open_.remove(at)
    return results


def grid_index(count):
    rows = lax.broadcasted_iota(jnp.int32, (count, count), 0)
    columns = lax.broadcasted_iota(jnp.int32, (count, count), 1)
    return rows, columns


def to_column(row, rows, columns):
    return jnp.sum(jnp.where(rows == columns, row, 0.0), axis=1, keepdims=True)


def to_row(column, rows, columns):
    return jnp.sum(jnp.where(rows == columns, column, 0.0), axis=0, keepdims=True)


def prepare(queries, raw_keys, values, base, gate_row):
    count = queries.shape[0]
    rows, columns = grid_index(count)
    raw = raw_keys.astype(F32)
    norm_inv = lax.rsqrt(jnp.sum(raw * raw, axis=1, keepdims=True) + 1e-06)
    keys = raw * norm_inv
    boost_row = base * gate_row
    rate_row = boost_row / (1.0 + boost_row)
    rate = to_column(rate_row, rows, columns)
    keys_s = split(keys)
    gram = dot(keys_s, keys_s, (1, 1))
    yield
    lower = jnp.where(rows // MB > columns // MB, gram * rate_row, 0.0)
    tile = min(count, 128)
    tile_rows, tile_columns = grid_index(tile)
    row_block, column_block = tile_rows // MB, tile_columns // MB
    eye = jnp.where(tile_rows == tile_columns, 1.0, 0.0)
    tiles = count // tile
    lowers = [lower[t * tile : (t + 1) * tile, t * tile : (t + 1) * tile] for t in range(tiles)]
    near = row_block // 2 == column_block // 2
    inverses = [eye - jnp.where(near, low, 0.0) for low in lowers]
    size = 2
    while size * MB < tile:
        here = (
            (row_block // (2 * size) == column_block // (2 * size))
            & (row_block // size > column_block // size)
        )
        inverses_s = [split(inv) for inv in inverses]
        middles = [dot(inv, split(jnp.where(here, low, 0.0))) for inv, low in zip(inverses_s, lowers)]
        yield
        inverses = [inv - dot(split(mid), inv_s) for inv, mid, inv_s in zip(inverses, middles, inverses_s)]
        yield
        size *= 2
    size = tile
    while size < count:
        joined = []
        for t in range(0, len(inverses), 2):
            low = lower[(t + 1) * size : (t + 2) * size, t * size : (t + 1) * size]
            first_s, second_s = split(inverses[t]), split(inverses[t + 1])
            middle = dot(second_s, split(low))
            yield
            corner = -dot(split(middle), first_s)
            yield
            joined.append(jnp.concatenate([
                jnp.concatenate([inverses[t], jnp.zeros((size, size), F32)], 1),
                jnp.concatenate([corner, inverses[t + 1]], 1),
            ], 0))
        inverses = joined
        size *= 2
    inverse_s = split(inverses[0])
    solved = dot(inverse_s, (jnp.concatenate([values, keys_s[0]], 1), jnp.concatenate([jnp.zeros_like(values), keys_s[1]], 1)))
    yield
    solved_s = split(solved)
    rate_keys_s = split(rate * keys)
    ends = dot(rate_keys_s, solved_s, (0, 0))
    return dict(
        norm_inv=norm_inv, keys=keys, keys_s=keys_s, boost_row=boost_row, rate=rate, rate_row=rate_row,
        inverse_s=inverse_s, solved=solved, solved_s=solved_s, ends=ends, rate_keys_s=rate_keys_s,
    )


def reach_out(queries, state):
    count, width = queries.shape
    rows, columns = grid_index(count)
    scores = jnp.where(rows >= columns, dot((queries, None), state["keys_s"], (1, 1)), 0.0)
    yield
    mixed = dot(split(scores * state["rate_row"]), state["solved_s"])
    yield
    state["scores_s"] = split(scores)
    state["reach_s"] = split(queries.astype(F32) - mixed[:, width:])
    state["own_out"] = mixed[:, :width]
    state["inverse_t"] = flipped(state["inverse_s"])
    state["pull_s"] = split(dot(state["inverse_t"], state["rate_keys_s"]))


def forward(start, gain, upstream, state):
    width = start.shape[0]
    start_s = split(start)
    inner_out = state["own_out"] + dot(state["reach_s"], start_s)
    yield
    solved_keys = (state["solved_s"][0][:, width:], state["solved_s"][1][:, width:])
    state["residual"] = state["solved"][:, :width] - dot(solved_keys, start_s)
    yield
    centred = inner_out - jnp.mean(inner_out, axis=1, keepdims=True)
    inv_std = lax.rsqrt(jnp.mean(centred * centred, axis=1, keepdims=True) + 1e-05)
    normed = centred * inv_std
    weighted = upstream * gain
    d_out = inv_std * (
        weighted
        - jnp.mean(weighted, axis=1, keepdims=True)
        - normed * jnp.mean(weighted * normed, axis=1, keepdims=True)
    )
    state["start_s"] = start_s
    state["d_out_s"] = split(d_out)
    state["d_gain"] = jnp.sum(upstream * normed, axis=0, keepdims=True)
    return dot(state["reach_s"], state["d_out_s"], (0, 0))


def query_grad(queries, upstream, state):
    rows, columns = grid_index(queries.shape[0])
    state["rate_res_s"] = split(state["rate"] * state["residual"])
    d_scores = jnp.where(rows >= columns, dot(state["d_out_s"], state["rate_res_s"], (1, 1)), 0.0)
    yield
    d_scores_s = split(d_scores)
    d_queries = upstream + dot(state["d_out_s"], state["start_s"], (1, 1)) + dot(d_scores_s, state["keys_s"])
    yield
    state["d_scores_s"] = d_scores_s
    return d_queries


def before_end(queries, state):
    state["from_scores"] = dot(state["d_scores_s"], (queries, None), (0, 0))
    yield
    pushed = state["rate"] * dot(state["scores_s"], state["d_out_s"], (0, 0))
    yield
    state["d_val"] = dot(state["inverse_t"], split(pushed))


def key_value_grad(end_grad, base, gate_row, state):
    rows, columns = grid_index(state["keys"].shape[0])
    end_s = split(end_grad)
    d_val = state["d_val"] + dot(state["pull_s"], end_s)
    yield
    d_val_s = split(d_val)
    strict = rows // MB > columns // MB
    d_lower = jnp.where(strict, dot(d_val_s, state["rate_res_s"], (1, 1)), 0.0)
    yield
    d_gram_s = split(d_lower + d_lower.T)
    d_keys = (
        state["from_scores"]
        - dot(d_val_s, state["start_s"], (1, 1))
        + dot(state["rate_res_s"], end_s, (1, 1))
        - dot(d_gram_s, state["keys_s"])
    )
    yield
    keys = state["keys"]
    d_raw = state["norm_inv"] * (d_keys - keys * jnp.sum(keys * d_keys, axis=1, keepdims=True))
    d_rate = jnp.sum(state["residual"] * d_val, axis=1, keepdims=True) / state["rate"]
    boost = state["boost_row"]
    d_boost = to_row(d_rate, rows, columns) / ((1.0 + boost) * (1.0 + boost))
    return d_raw, d_val, d_boost * base, jnp.sum(d_boost * gate_row, axis=1, keepdims=True)


def kernel(
    sizes,
    tok_ref, w_hbm, init_ref, rates_ref, gate_ref, gain_ref, cot_ref,
    gt_out, proj_out, ext_out, gates_out,
    w_ref, tok_t, maps, maps_all, pulls, pulls_all, acc, ext, landing, ext_landing, part, from_low, from_high,
    maps_send, maps_recv, pulls_send, pulls_recv, up_send, up_recv, down_send, down_recv, red_send, red_recv, w_sem,
):
    n_dp, n_ctx, n_head = sizes
    count, model = tok_ref.shape
    heads, width, _ = init_ref.shape
    dp, ctx, head = lax.axis_index("dp"), lax.axis_index("ctx"), lax.axis_index("head")
    place = {"dp": dp, "ctx": ctx}
    w_copies = [pltpu.make_async_copy(w_hbm.at[which], w_ref.at[which], w_sem.at[which]) for which in (1, 2, 0)]
    for copy in w_copies:
        copy.start()

    def flip(axis, bit):
        step = 1 << bit
        mine = lax.rem(place[axis] // step, 2)
        return mine, place[axis] + step - 2 * step * mine

    dp_bits = [("dp", b) for b in range(n_dp.bit_length() - 1)]
    ctx_bits = [("ctx", b) for b in range(n_ctx.bit_length() - 1)]
    orders = (ctx_bits + dp_bits, ctx_bits[:1] + dp_bits + ctx_bits[1:])
    stages = len(orders[0])

    barrier = pltpu.get_barrier_semaphore()
    for off in range(1, n_ctx):
        pl.semaphore_signal(barrier, inc=1, device_id={"ctx": lax.rem(ctx + off, n_ctx)}, device_id_type=MESH)
    for off in range(1, n_head):
        pl.semaphore_signal(barrier, inc=1, device_id={"head": lax.rem(head + off, n_head)}, device_id_type=MESH)
    for axis, bit in dp_bits:
        pl.semaphore_signal(barrier, inc=1, device_id={axis: flip(axis, bit)[1]}, device_id_type=MESH)

    tokens = tok_ref[...]
    projected = [None] * 3
    for which in (1, 2, 0):
        w_copies[(1, 2, 0).index(which)].wait()
        projected[which] = jnp.dot(tokens, w_ref[which], preferred_element_type=F32).astype(BF16)
    span = [slice(h * width, (h + 1) * width) for h in range(heads)]
    queries = [projected[0][:, s] for s in span]
    rows, columns = grid_index(width)
    eye = jnp.where(rows == columns, 1.0, 0.0)
    states = together([
        prepare(
            queries[h], projected[1][:, span[h]], projected[2][:, span[h]], rates_ref[h], gate_ref[0, h : h + 1, :]
        )
        for h in range(heads)
    ])
    for h in range(heads):
        maps[h, 0] = eye - states[h]["ends"][:, width:]
        maps[h, 1] = states[h]["ends"][:, :width]

    pl.semaphore_wait(barrier, (n_ctx - 1) + (n_head - 1) + len(dp_bits))

    def share(block, slots, send, recv):
        slots[pl.ds(ctx, 1)] = block[...][None]
        copies = []
        for off in range(1, n_ctx):
            copy = pltpu.make_async_remote_copy(
                src_ref=block, dst_ref=slots.at[ctx], send_sem=send.at[off - 1], recv_sem=recv.at[off - 1],
                device_id={"ctx": lax.rem(ctx + off, n_ctx)}, device_id_type=MESH,
            )
            copy.start()
            copies.append(copy)
        return copies

    copies = share(maps, maps_all, maps_send, maps_recv)
    together([reach_out(queries[h], states[h]) for h in range(heads)])
    tok_t[...] = tokens.T
    for copy in copies:
        copy.wait()

    starts = [init_ref[h] for h in range(heads)]
    for i in range(n_ctx - 1):
        for h in range(heads):
            moved = dot(split(maps_all[i, h, 0]), split(starts[h])) + maps_all[i, h, 1]
            starts[h] = jnp.where(ctx > i, moved, starts[h])
    upstreams = [cot_ref[:, span[h]].astype(F32) for h in range(heads)]
    pulled = together([
        forward(starts[h], gain_ref[h : h + 1, :], upstreams[h], states[h]) for h in range(heads)
    ])
    for h in range(heads):
        pulls[h] = pulled[h]
    copies = share(pulls, pulls_all, pulls_send, pulls_recv)

    half = model // 2
    work = [(which * 2 + part_, acc, proj_out, landing, (which * 2 + part_) * half, half, orders[part_]) for which in range(3) for part_ in range(2)]
    work.append((6, ext, ext_out, ext_landing, 0, ext.shape[0], orders[0]))
    at = {item[0]: item[4] for item in work}
    flight = {}

    def reduce_start(item, stage):
        number, source, _, land, base, length, order = item
        axis, bit = order[stage]
        mine, partner = flip(axis, bit)
        length = length >> (stage + 1)
        slot = (0 if number == 6 else number * half) + (item[5] - (item[5] >> stage))
        away = pl.multiple_of(at[number] + (1 - mine) * length, 8)
        copy = pltpu.make_async_remote_copy(
            src_ref=source.at[pl.ds(away, length)], dst_ref=land.at[pl.ds(slot, length)],
            send_sem=red_send.at[number, stage], recv_sem=red_recv.at[number, stage],
            device_id={axis: partner}, device_id_type=MESH,
        )
        copy.start()
        flight[number] = (copy, slot, length)
        at[number] = pl.multiple_of(at[number] + mine * length, 8)

    def reduce_end(item, stage):
        number, source, target, land = item[:4]
        copy, slot, length = flight[number]
        copy.wait()
        total = source[pl.ds(at[number], length)] + land[pl.ds(slot, length)]
        (target if stage == stages - 1 else source)[pl.ds(at[number], length)] = total

    def gather_start(item, stage):
        number, _, target, _, _, length, order = item
        axis, bit = order[stage]
        mine, partner = flip(axis, bit)
        length = length >> (stage + 1)
        window = target.at[pl.ds(at[number], length)]
        copy = pltpu.make_async_remote_copy(
            src_ref=window, dst_ref=window,
            send_sem=red_send.at[number, 2 * stages - 1 - stage], recv_sem=red_recv.at[number, 2 * stages - 1 - stage],
            device_id={axis: partner}, device_id_type=MESH,
        )
        copy.start()
        flight[number] = (copy, None, None)
        at[number] = pl.multiple_of(at[number] - mine * length, 8)

    def project(which, grads):
        grad = jnp.concatenate(grads, axis=1).astype(BF16)
        for part_ in range(2):
            where = pl.ds((which * 2 + part_) * half, half)
            acc[where] = jnp.dot(tok_t[pl.ds(part_ * half, half)], grad, preferred_element_type=F32)
            reduce_start(work[which * 2 + part_], 0)
        return grad

    def advance(item, turn):
        if turn < stages:
            reduce_end(item, turn)
        else:
            flight[item[0]][0].wait()
        if turn + 1 < stages:
            reduce_start(item, turn + 1)
        elif turn + 1 < 2 * stages:
            gather_start(item, 2 * stages - 2 - turn)

    share_ = model // n_head
    d_rows = [None] * 3

    def token_part(which_head, which):
        weight = w_ref[which, which_head * share_ : (which_head + 1) * share_, :]
        return lax.dot_general(d_rows[which], weight, (((1,), (1,)), ((), ())), preferred_element_type=F32)

    def upward(j):
        return pltpu.make_async_remote_copy(
            src_ref=part.at[j], dst_ref=from_low.at[j], send_sem=up_send.at[j], recv_sem=up_recv.at[j],
            device_id={"head": lax.rem(head + 1, n_head)}, device_id_type=MESH,
        )

    def downward(j):
        return pltpu.make_async_remote_copy(
            src_ref=part.at[j], dst_ref=from_high.at[j], send_sem=down_send.at[j], recv_sem=down_recv.at[j],
            device_id={"head": lax.rem(head + n_head - 1, n_head)}, device_id_type=MESH,
        )

    def pass_on(turn):
        for j in range(n_head):
            low = turn - (n_head - 1 - j)
            if 1 <= low <= j:

                @pl.when(head == low)
                def _():
                    upward(j).wait_recv()
                    if low < j:
                        part[j] = part[j] + from_low[j]
                        upward(j).start()

            high = n_head - 1 - (turn - j)
            if j <= high <= n_head - 2:

                @pl.when(head == high)
                def _():
                    downward(j).wait_recv()
                    if high > j:
                        part[j] = part[j] + from_high[j]
                        downward(j).start()

    d_rows[0] = project(0, together([query_grad(queries[h], upstreams[h], states[h]) for h in range(heads)]))
    together([before_end(queries[h], states[h]) for h in range(heads)])
    for j in range(n_head):
        part[j] = token_part(j, 0)
    for item in work[:2]:
        advance(item, 0)
    for copy in copies:
        copy.wait()

    grads = [jnp.zeros((width, width), F32)] * heads
    end_grads = list(grads)
    for i in reversed(range(n_ctx)):
        for h in range(heads):
            end_grads[h] = jnp.where(ctx == i, grads[h], end_grads[h])
            grads[h] = dot(split(maps_all[i, h, 0]), split(grads[h]), (0, 0)) + pulls_all[i, h]
    results = together([
        key_value_grad(end_grads[h], rates_ref[h], gate_ref[0, h : h + 1, :], states[h]) for h in range(heads)
    ])
    d_rows[1] = project(1, [r[0] for r in results])
    d_rows[2] = project(2, [r[1] for r in results])
    for item in work[:2]:
        advance(item, 1)

    for item in work[2:4]:
        advance(item, 0)
    for j in range(n_head):
        part[j] = part[j] + token_part(j, 1) + token_part(j, 2)

    @pl.when(head == 0)
    def _():
        for j in range(n_head - 1, 0, -1):
            upward(j).start()

    @pl.when(head == n_head - 1)
    def _():
        for j in range(n_head - 1):
            downward(j).start()

    for item in work[4:6]:
        advance(item, 0)

    ext[...] = jnp.zeros_like(ext)
    for h in range(heads):
        ext[0:width, span[h]] = jnp.where(ctx == 0, grads[h], 0.0)
        gates_out[0, h : h + 1, :] = results[h][2]
        ext[width : width + 1, span[h]] = states[h]["d_gain"]
        ext[width + 8 : width + 9, span[h]] = jnp.broadcast_to(results[h][3], (1, width))
    reduce_start(work[6], 0)
    last = 2 * stages - 1
    passed = 0
    for turn in range(1, last + 1):
        if turn < last:
            for item in work[:2]:
                advance(item, turn + 1)
        for item in work[2:6]:
            advance(item, turn)
        advance(work[6], turn - 1)
        if turn in (1, 3, 4):
            passed += 1
            pass_on(passed)
    for turn in range(passed + 1, n_head):
        pass_on(turn)
    for j in range(n_head):

        @pl.when(head == j)
        def _():
            total = part[j]
            if j > 0:
                total = total + from_low[j]
            if j < n_head - 1:
                total = total + from_high[j]
            gt_out[...] = total.astype(BF16)

        @pl.when(head < j)
        def _():
            upward(j).wait_send()

        @pl.when(head > j)
        def _():
            downward(j).wait_send()

    advance(work[6], last)


def finish_kernel(gt_in, proj_in, ext_in, gates_in, gt_out, proj_out, init_out, gain_out, rates_out, gates_out, sem):
    copy = pltpu.make_async_copy(proj_in, proj_out, sem)
    copy.start()
    heads, width, _ = init_out.shape
    gt_out[...] = gt_in[...]
    gates_out[...] = gates_in[...]
    for h in range(heads):
        span = slice(h * width, (h + 1) * width)
        init_out[h] = ext_in[0:width, span]
        gain_out[h : h + 1, :] = ext_in[width : width + 1, span]
        rates_out[h] = jnp.max(ext_in[width + 8 : width + 9, span])
    copy.wait()


def body(sizes, tokens, proj_weights, init_weight, base_rates, gate_values, out_gain, cotangent):
    flattened = tokens.reshape(-1, tokens.shape[-1])
    count, model = flattened.shape
    heads, width, _ = init_weight.shape
    n_dp, n_ctx, n_head = sizes
    stages = (n_dp * n_ctx).bit_length() - 1
    span = heads * width
    ext_rows = 256
    vmem, dma = pltpu.VMEM, pltpu.SemaphoreType.DMA
    in_vmem = pl.BlockSpec(memory_space=vmem)
    tokens_grad, proj, ext, gates = pl.pallas_call(
        functools.partial(kernel, sizes),
        out_shape=(
            vmem((count, model // n_head), BF16),
            vmem((3 * model, span), F32),
            vmem((ext_rows, span), F32),
            vmem(gate_values.shape, F32),
        ),
        in_specs=[in_vmem, pl.BlockSpec(memory_space=pltpu.HBM), in_vmem] + [pl.BlockSpec(memory_space=pltpu.SMEM)] + [in_vmem] * 3,
        out_specs=(in_vmem,) * 4,
        scratch_shapes=[
            vmem(proj_weights.shape, BF16),
            vmem((model, count), BF16),
            vmem((heads, 2, width, width), F32),
            vmem((n_ctx, heads, 2, width, width), F32),
            vmem((heads, width, width), F32),
            vmem((n_ctx, heads, width, width), F32),
            vmem((3 * model, span), F32),
            vmem((ext_rows, span), F32),
            vmem((3 * model, span), F32),
            vmem((ext_rows, span), F32),
            vmem((n_head, count, model // n_head), F32),
            vmem((n_head, count, model // n_head), F32),
            vmem((n_head, count, model // n_head), F32),
            dma((n_ctx - 1,)), dma((n_ctx - 1,)), dma((n_ctx - 1,)), dma((n_ctx - 1,)),
            dma((n_head,)), dma((n_head,)), dma((n_head,)), dma((n_head,)),
            dma((7, 2 * stages)), dma((7, 2 * stages)), dma((3,)),
        ],
        compiler_params=pltpu.CompilerParams(
            collective_id=0, has_side_effects=True, vmem_limit_bytes=44 * 1024 * 1024
        ),
        cost_estimate=pl.CostEstimate(flops=4_000_000_000, bytes_accessed=12_000_000, transcendentals=0),
    )(*(
        pltpu.with_memory_space_constraint(x, pltpu.HBM)
        for x in (
            flattened, proj_weights, init_weight, base_rates, gate_values, out_gain,
            cotangent.reshape(count, span),
        )
    ))
    anywhere = pl.BlockSpec(memory_space=pl.ANY)
    tokens_grad, proj, grad_init, grad_gain, grad_rates, gates = pl.pallas_call(
        finish_kernel,
        out_shape=(
            jax.ShapeDtypeStruct((count, model // n_head), BF16),
            jax.ShapeDtypeStruct((3 * model, span), F32),
            jax.ShapeDtypeStruct(init_weight.shape, F32),
            jax.ShapeDtypeStruct(out_gain.shape, F32),
            jax.ShapeDtypeStruct((heads,), F32),
            jax.ShapeDtypeStruct(gate_values.shape, F32),
        ),
        in_specs=[in_vmem] * 4,
        out_specs=(in_vmem, anywhere, in_vmem, in_vmem, pl.BlockSpec(memory_space=pltpu.SMEM), in_vmem),
        scratch_shapes=[dma],
        compiler_params=pltpu.CompilerParams(vmem_limit_bytes=12 * 1024 * 1024),
        cost_estimate=pl.CostEstimate(flops=0, bytes_accessed=8_000_000, transcendentals=0),
    )(*(pltpu.with_memory_space_constraint(x, pltpu.VMEM) for x in (tokens_grad, proj, ext, gates)))
    return (
        tokens_grad[None], proj.reshape(3, model, span), grad_init, grad_gain, grad_rates, gates,
    )


def solution(mesh):
    sizes = (mesh.shape["dp"], mesh.shape["ctx"], mesh.shape["head"])
    in_specs = (
        P("dp", "ctx", None),
        P(None, None, "head"),
        P("head", None, None),
        P("head"),
        P("dp", "head", "ctx"),
        P("head", None),
        P("dp", "ctx", "head"),
    )
    out_specs = (
        P("dp", "ctx", "head"),
        P(None, None, "head"),
        P("head", None, None),
        P("head", None),
        P("head"),
        P("dp", "head", "ctx"),
    )
    return jax.shard_map(
        functools.partial(body, sizes), mesh=mesh, in_specs=in_specs, out_specs=out_specs, check_vma=False
    )
```

```python
import functools

import jax
import jax.numpy as jnp
from jax import lax
from jax.experimental import pallas as pl
from jax.experimental.pallas import tpu as pltpu
from jax.sharding import PartitionSpec as P

MB = 16
F32 = jnp.float32
BF16 = jnp.bfloat16
MESH = pl.DeviceIdType.MESH


def split(x):
    if x.dtype == BF16:
        return (x, None)
    high = x.astype(BF16)
    return (high, (x - high.astype(F32)).astype(BF16))


def flipped(x):
    return tuple(None if piece is None else piece.T for piece in x)


def dot(left, right, dims=(1, 0)):
    if dims[0] == 0:
        return dot(flipped(left), right, (1, dims[1]))
    terms = [(left[0], right[0])]
    if right[1] is not None:
        terms.append((left[0], right[1]))
    if left[1] is not None:
        terms.append((left[1], right[0]))
    a = jnp.concatenate([t[0] for t in terms], axis=1)
    b = jnp.concatenate([t[1] for t in terms], axis=dims[1])
    return lax.dot_general(a, b, (((1,), (dims[1],)), ((), ())), preferred_element_type=F32)


def together(steps):
    results = [None] * len(steps)
    open_ = list(range(len(steps)))
    while open_:
        for at in list(open_):
            try:
                next(steps[at])
            except StopIteration as end:
                results[at] = end.value
                open_.remove(at)
    return results


def grid_index(count):
    rows = lax.broadcasted_iota(jnp.int32, (count, count), 0)
    columns = lax.broadcasted_iota(jnp.int32, (count, count), 1)
    return rows, columns


def to_column(row, rows, columns):
    return jnp.sum(jnp.where(rows == columns, row, 0.0), axis=1, keepdims=True)


def to_row(column, rows, columns):
    return jnp.sum(jnp.where(rows == columns, column, 0.0), axis=0, keepdims=True)


def prepare(queries, raw_keys, values, base, gate_row):
    count = queries.shape[0]
    rows, columns = grid_index(count)
    raw = raw_keys.astype(F32)
    norm_inv = lax.rsqrt(jnp.sum(raw * raw, axis=1, keepdims=True) + 1e-06)
    keys = raw * norm_inv
    boost_row = base * gate_row
    rate_row = boost_row / (1.0 + boost_row)
    rate = to_column(rate_row, rows, columns)
    keys_s = split(keys)
    gram = dot(keys_s, keys_s, (1, 1))
    yield
    lower = jnp.where(rows // MB > columns // MB, gram * rate_row, 0.0)
    tile = min(count, 128)
    tile_rows, tile_columns = grid_index(tile)
    row_block, column_block = tile_rows // MB, tile_columns // MB
    eye = jnp.where(tile_rows == tile_columns, 1.0, 0.0)
    tiles = count // tile
    lowers = [lower[t * tile : (t + 1) * tile, t * tile : (t + 1) * tile] for t in range(tiles)]
    near = row_block // 2 == column_block // 2
    inverses = [eye - jnp.where(near, low, 0.0) for low in lowers]
    size = 2
    while size * MB < tile:
        here = (
            (row_block // (2 * size) == column_block // (2 * size))
            & (row_block // size > column_block // size)
        )
        inverses_s = [split(inv) for inv in inverses]
        middles = [dot(inv, split(jnp.where(here, low, 0.0))) for inv, low in zip(inverses_s, lowers)]
        yield
        inverses = [inv - dot(split(mid), inv_s) for inv, mid, inv_s in zip(inverses, middles, inverses_s)]
        yield
        size *= 2
    size = tile
    while size < count:
        joined = []
        for t in range(0, len(inverses), 2):
            low = lower[(t + 1) * size : (t + 2) * size, t * size : (t + 1) * size]
            first_s, second_s = split(inverses[t]), split(inverses[t + 1])
            middle = dot(second_s, split(low))
            yield
            corner = -dot(split(middle), first_s)
            yield
            joined.append(jnp.concatenate([
                jnp.concatenate([inverses[t], jnp.zeros((size, size), F32)], 1),
                jnp.concatenate([corner, inverses[t + 1]], 1),
            ], 0))
        inverses = joined
        size *= 2
    inverse_s = split(inverses[0])
    solved = dot(inverse_s, (jnp.concatenate([values, keys_s[0]], 1), jnp.concatenate([jnp.zeros_like(values), keys_s[1]], 1)))
    yield
    solved_s = split(solved)
    rate_keys_s = split(rate * keys)
    ends = dot(rate_keys_s, solved_s, (0, 0))
    return dict(
        norm_inv=norm_inv, keys=keys, keys_s=keys_s, boost_row=boost_row, rate=rate, rate_row=rate_row,
        inverse_s=inverse_s, solved=solved, solved_s=solved_s, ends=ends, rate_keys_s=rate_keys_s,
    )


def reach_out(queries, state):
    count, width = queries.shape
    rows, columns = grid_index(count)
    scores = jnp.where(rows >= columns, dot((queries, None), state["keys_s"], (1, 1)), 0.0)
    yield
    mixed = dot(split(scores * state["rate_row"]), state["solved_s"])
    yield
    state["scores_s"] = split(scores)
    state["reach_s"] = split(queries.astype(F32) - mixed[:, width:])
    state["own_out"] = mixed[:, :width]
    state["inverse_t"] = flipped(state["inverse_s"])
    state["pull_s"] = split(dot(state["inverse_t"], state["rate_keys_s"]))


def forward(start, gain, upstream, state):
    width = start.shape[0]
    start_s = split(start)
    inner_out = state["own_out"] + dot(state["reach_s"], start_s)
    yield
    solved_keys = (state["solved_s"][0][:, width:], state["solved_s"][1][:, width:])
    state["residual"] = state["solved"][:, :width] - dot(solved_keys, start_s)
    yield
    centred = inner_out - jnp.mean(inner_out, axis=1, keepdims=True)
    inv_std = lax.rsqrt(jnp.mean(centred * centred, axis=1, keepdims=True) + 1e-05)
    normed = centred * inv_std
    weighted = upstream * gain
    d_out = inv_std * (
        weighted
        - jnp.mean(weighted, axis=1, keepdims=True)
        - normed * jnp.mean(weighted * normed, axis=1, keepdims=True)
    )
    state["start_s"] = start_s
    state["d_out_s"] = split(d_out)
    state["d_gain"] = jnp.sum(upstream * normed, axis=0, keepdims=True)
    return dot(state["reach_s"], state["d_out_s"], (0, 0))


def query_grad(queries, upstream, state):
    rows, columns = grid_index(queries.shape[0])
    state["rate_res_s"] = split(state["rate"] * state["residual"])
    d_scores = jnp.where(rows >= columns, dot(state["d_out_s"], state["rate_res_s"], (1, 1)), 0.0)
    yield
    d_scores_s = split(d_scores)
    d_queries = upstream + dot(state["d_out_s"], state["start_s"], (1, 1)) + dot(d_scores_s, state["keys_s"])
    yield
    state["d_scores_s"] = d_scores_s
    return d_queries


def before_end(queries, state):
    state["from_scores"] = dot(state["d_scores_s"], (queries, None), (0, 0))
    yield
    pushed = state["rate"] * dot(state["scores_s"], state["d_out_s"], (0, 0))
    yield
    state["d_val"] = dot(state["inverse_t"], split(pushed))


def key_value_grad(end_grad, base, gate_row, state):
    rows, columns = grid_index(state["keys"].shape[0])
    end_s = split(end_grad)
    d_val = state["d_val"] + dot(state["pull_s"], end_s)
    yield
    d_val_s = split(d_val)
    strict = rows // MB > columns // MB
    d_lower = jnp.where(strict, dot(d_val_s, state["rate_res_s"], (1, 1)), 0.0)
    yield
    d_gram_s = split(d_lower + d_lower.T)
    d_keys = (
        state["from_scores"]
        - dot(d_val_s, state["start_s"], (1, 1))
        + dot(state["rate_res_s"], end_s, (1, 1))
        - dot(d_gram_s, state["keys_s"])
    )
    yield
    keys = state["keys"]
    d_raw = state["norm_inv"] * (d_keys - keys * jnp.sum(keys * d_keys, axis=1, keepdims=True))
    d_rate = jnp.sum(state["residual"] * d_val, axis=1, keepdims=True) / state["rate"]
    boost = state["boost_row"]
    d_boost = to_row(d_rate, rows, columns) / ((1.0 + boost) * (1.0 + boost))
    return d_raw, d_val, d_boost * base, jnp.sum(d_boost * gate_row, axis=1, keepdims=True)


def kernel(
    sizes,
    tok_ref, w_hbm, init_ref, rates_ref, gate_ref, gain_ref, cot_ref,
    gt_out, proj_out, ext_out, gates_out,
    w_ref, tok_t, maps, maps_all, pulls, pulls_all, acc, ext, landing, ext_landing, part, from_low, from_high,
    maps_send, maps_recv, pulls_send, pulls_recv, up_send, up_recv, down_send, down_recv, red_send, red_recv, w_sem,
):
    n_dp, n_ctx, n_head = sizes
    count, model = tok_ref.shape
    heads, width, _ = init_ref.shape
    dp, ctx, head = lax.axis_index("dp"), lax.axis_index("ctx"), lax.axis_index("head")
    place = {"dp": dp, "ctx": ctx}
    w_copies = [pltpu.make_async_copy(w_hbm.at[which], w_ref.at[which], w_sem.at[which]) for which in (1, 2, 0)]
    for copy in w_copies:
        copy.start()

    def flip(axis, bit):
        step = 1 << bit
        mine = lax.rem(place[axis] // step, 2)
        return mine, place[axis] + step - 2 * step * mine

    dp_bits = [("dp", b) for b in range(n_dp.bit_length() - 1)]
    ctx_bits = [("ctx", b) for b in range(n_ctx.bit_length() - 1)]
    orders = (ctx_bits + dp_bits, ctx_bits[:1] + dp_bits + ctx_bits[1:])
    stages = len(orders[0])

    barrier = pltpu.get_barrier_semaphore()
    for off in range(1, n_ctx):
        pl.semaphore_signal(barrier, inc=1, device_id={"ctx": lax.rem(ctx + off, n_ctx)}, device_id_type=MESH)
    for off in range(1, n_head):
        pl.semaphore_signal(barrier, inc=1, device_id={"head": lax.rem(head + off, n_head)}, device_id_type=MESH)
    for axis, bit in dp_bits:
        pl.semaphore_signal(barrier, inc=1, device_id={axis: flip(axis, bit)[1]}, device_id_type=MESH)

    tokens = tok_ref[...]
    projected = [None] * 3
    for which in (1, 2, 0):
        w_copies[(1, 2, 0).index(which)].wait()
        projected[which] = jnp.dot(tokens, w_ref[which], preferred_element_type=F32).astype(BF16)
    span = [slice(h * width, (h + 1) * width) for h in range(heads)]
    queries = [projected[0][:, s] for s in span]
    rows, columns = grid_index(width)
    eye = jnp.where(rows == columns, 1.0, 0.0)
    states = together([
        prepare(
            queries[h], projected[1][:, span[h]], projected[2][:, span[h]], rates_ref[h], gate_ref[0, h : h + 1, :]
        )
        for h in range(heads)
    ])
    for h in range(heads):
        maps[h, 0] = eye - states[h]["ends"][:, width:]
        maps[h, 1] = states[h]["ends"][:, :width]

    pl.semaphore_wait(barrier, (n_ctx - 1) + (n_head - 1) + len(dp_bits))

    def share(block, slots, send, recv):
        slots[pl.ds(ctx, 1)] = block[...][None]
        copies = []
        for off in range(1, n_ctx):
            copy = pltpu.make_async_remote_copy(
                src_ref=block, dst_ref=slots.at[ctx], send_sem=send.at[off - 1], recv_sem=recv.at[off - 1],
                device_id={"ctx": lax.rem(ctx + off, n_ctx)}, device_id_type=MESH,
            )
            copy.start()
            copies.append(copy)
        return copies

    copies = share(maps, maps_all, maps_send, maps_recv)
    together([reach_out(queries[h], states[h]) for h in range(heads)])
    tok_t[...] = tokens.T
    sent = list(copies)
    for copy in copies:
        copy.wait_recv()

    starts = [init_ref[h] for h in range(heads)]
    for i in range(n_ctx - 1):
        for h in range(heads):
            moved = dot(split(maps_all[i, h, 0]), split(starts[h])) + maps_all[i, h, 1]
            starts[h] = jnp.where(ctx > i, moved, starts[h])
    upstreams = [cot_ref[:, span[h]].astype(F32) for h in range(heads)]
    pulled = together([
        forward(starts[h], gain_ref[h : h + 1, :], upstreams[h], states[h]) for h in range(heads)
    ])
    for h in range(heads):
        pulls[h] = pulled[h]
    copies = share(pulls, pulls_all, pulls_send, pulls_recv)

    half = model // 2
    work = [(which * 2 + part_, acc, proj_out, landing, (which * 2 + part_) * half, half, orders[part_]) for which in range(3) for part_ in range(2)]
    work.append((6, ext, ext_out, ext_landing, 0, ext.shape[0], orders[0]))
    at = {item[0]: item[4] for item in work}
    flight = {}

    def reduce_start(item, stage):
        number, source, _, land, base, length, order = item
        axis, bit = order[stage]
        mine, partner = flip(axis, bit)
        length = length >> (stage + 1)
        slot = (0 if number == 6 else number * half) + (item[5] - (item[5] >> stage))
        away = pl.multiple_of(at[number] + (1 - mine) * length, 8)
        copy = pltpu.make_async_remote_copy(
            src_ref=source.at[pl.ds(away, length)], dst_ref=land.at[pl.ds(slot, length)],
            send_sem=red_send.at[number, stage], recv_sem=red_recv.at[number, stage],
            device_id={axis: partner}, device_id_type=MESH,
        )
        copy.start()
        flight[number] = (copy, slot, length)
        at[number] = pl.multiple_of(at[number] + mine * length, 8)

    def reduce_end(item, stage):
        number, source, target, land = item[:4]
        copy, slot, length = flight[number]
        copy.wait_recv()
        sent.append(copy)
        total = source[pl.ds(at[number], length)] + land[pl.ds(slot, length)]
        (target if stage == stages - 1 else source)[pl.ds(at[number], length)] = total

    def gather_start(item, stage):
        number, _, target, _, _, length, order = item
        axis, bit = order[stage]
        mine, partner = flip(axis, bit)
        length = length >> (stage + 1)
        window = target.at[pl.ds(at[number], length)]
        copy = pltpu.make_async_remote_copy(
            src_ref=window, dst_ref=window,
            send_sem=red_send.at[number, 2 * stages - 1 - stage], recv_sem=red_recv.at[number, 2 * stages - 1 - stage],
            device_id={axis: partner}, device_id_type=MESH,
        )
        copy.start()
        flight[number] = (copy, None, None)
        at[number] = pl.multiple_of(at[number] - mine * length, 8)

    def project(which, grads):
        grad = jnp.concatenate(grads, axis=1).astype(BF16)
        for part_ in range(2):
            where = pl.ds((which * 2 + part_) * half, half)
            acc[where] = jnp.dot(tok_t[pl.ds(part_ * half, half)], grad, preferred_element_type=F32)
            reduce_start(work[which * 2 + part_], 0)
        return grad

    def advance(item, turn):
        if turn < stages:
            reduce_end(item, turn)
        else:
            flight[item[0]][0].wait_recv()
            sent.append(flight[item[0]][0])
        if turn + 1 < stages:
            reduce_start(item, turn + 1)
        elif turn + 1 < 2 * stages:
            gather_start(item, 2 * stages - 2 - turn)

    share_ = model // n_head
    d_rows = [None] * 3

    def token_part(which_head, which):
        weight = w_ref[which, which_head * share_ : (which_head + 1) * share_, :]
        return lax.dot_general(d_rows[which], weight, (((1,), (1,)), ((), ())), preferred_element_type=F32)

    def upward(j):
        return pltpu.make_async_remote_copy(
            src_ref=part.at[j], dst_ref=from_low.at[j], send_sem=up_send.at[j], recv_sem=up_recv.at[j],
            device_id={"head": lax.rem(head + 1, n_head)}, device_id_type=MESH,
        )

    def downward(j):
        return pltpu.make_async_remote_copy(
            src_ref=part.at[j], dst_ref=from_high.at[j], send_sem=down_send.at[j], recv_sem=down_recv.at[j],
            device_id={"head": lax.rem(head + n_head - 1, n_head)}, device_id_type=MESH,
        )

    def pass_on(turn):
        for j in range(n_head):
            low = turn - (n_head - 1 - j)
            if 1 <= low <= j:

                @pl.when(head == low)
                def _():
                    upward(j).wait_recv()
                    if low < j:
                        part[j] = part[j] + from_low[j]
                        upward(j).start()

            high = n_head - 1 - (turn - j)
            if j <= high <= n_head - 2:

                @pl.when(head == high)
                def _():
                    downward(j).wait_recv()
                    if high > j:
                        part[j] = part[j] + from_high[j]
                        downward(j).start()

    d_rows[0] = project(0, together([query_grad(queries[h], upstreams[h], states[h]) for h in range(heads)]))
    together([before_end(queries[h], states[h]) for h in range(heads)])
    for j in range(n_head):
        part[j] = token_part(j, 0)
    for item in work[:2]:
        advance(item, 0)
    sent.extend(copies)
    for copy in copies:
        copy.wait_recv()

    grads = [jnp.zeros((width, width), F32)] * heads
    end_grads = list(grads)
    for i in reversed(range(n_ctx)):
        for h in range(heads):
            end_grads[h] = jnp.where(ctx == i, grads[h], end_grads[h])
            grads[h] = dot(split(maps_all[i, h, 0]), split(grads[h]), (0, 0)) + pulls_all[i, h]
    results = together([
        key_value_grad(end_grads[h], rates_ref[h], gate_ref[0, h : h + 1, :], states[h]) for h in range(heads)
    ])
    d_rows[1] = project(1, [r[0] for r in results])
    d_rows[2] = project(2, [r[1] for r in results])
    for item in work[:2]:
        advance(item, 1)

    for item in work[2:4]:
        advance(item, 0)
    for j in range(n_head):
        part[j] = part[j] + token_part(j, 1) + token_part(j, 2)

    @pl.when(head == 0)
    def _():
        for j in range(n_head - 1, 0, -1):
            upward(j).start()

    @pl.when(head == n_head - 1)
    def _():
        for j in range(n_head - 1):
            downward(j).start()

    for item in work[4:6]:
        advance(item, 0)

    ext[...] = jnp.zeros_like(ext)
    for h in range(heads):
        ext[0:width, span[h]] = jnp.where(ctx == 0, grads[h], 0.0)
        gates_out[0, h : h + 1, :] = results[h][2]
        ext[width : width + 1, span[h]] = states[h]["d_gain"]
        ext[width + 8 : width + 9, span[h]] = jnp.broadcast_to(results[h][3], (1, width))
    reduce_start(work[6], 0)
    last = 2 * stages - 1
    passed = 0
    for turn in range(1, last + 1):
        if turn < last:
            for item in work[:2]:
                advance(item, turn + 1)
        for item in work[2:6]:
            advance(item, turn)
        advance(work[6], turn - 1)
        if turn in (1, 3, 4):
            passed += 1
            pass_on(passed)
    for turn in range(passed + 1, n_head):
        pass_on(turn)
    for j in range(n_head):

        @pl.when(head == j)
        def _():
            total = part[j]
            if j > 0:
                total = total + from_low[j]
            if j < n_head - 1:
                total = total + from_high[j]
            gt_out[...] = total.astype(BF16)

        @pl.when(head < j)
        def _():
            upward(j).wait_send()

        @pl.when(head > j)
        def _():
            downward(j).wait_send()

    advance(work[6], last)
    for copy in sent:
        copy.wait_send()


def finish_kernel(gt_in, proj_in, ext_in, gates_in, gt_out, proj_out, init_out, gain_out, rates_out, gates_out, sem):
    pieces = sem.shape[0]
    rows = proj_in.shape[0] // pieces
    copies = []
    for n in range(pieces):
        where = pl.ds(n * rows, rows)
        copies.append(pltpu.make_async_copy(proj_in.at[where], proj_out.at[where], sem.at[n]))
        copies[n].start()
    heads, width, _ = init_out.shape
    gt_out[...] = gt_in[...]
    gates_out[...] = gates_in[...]
    for h in range(heads):
        span = slice(h * width, (h + 1) * width)
        init_out[h] = ext_in[0:width, span]
        gain_out[h : h + 1, :] = ext_in[width : width + 1, span]
        rates_out[h] = jnp.max(ext_in[width + 8 : width + 9, span])
    for copy in copies:
        copy.wait()


def body(sizes, tokens, proj_weights, init_weight, base_rates, gate_values, out_gain, cotangent):
    flattened = tokens.reshape(-1, tokens.shape[-1])
    count, model = flattened.shape
    heads, width, _ = init_weight.shape
    n_dp, n_ctx, n_head = sizes
    stages = (n_dp * n_ctx).bit_length() - 1
    span = heads * width
    ext_rows = 256
    vmem, dma = pltpu.VMEM, pltpu.SemaphoreType.DMA
    in_vmem = pl.BlockSpec(memory_space=vmem)
    tokens_grad, proj, ext, gates = pl.pallas_call(
        functools.partial(kernel, sizes),
        out_shape=(
            vmem((count, model // n_head), BF16),
            vmem((3 * model, span), F32),
            vmem((ext_rows, span), F32),
            vmem(gate_values.shape, F32),
        ),
        in_specs=[in_vmem, pl.BlockSpec(memory_space=pltpu.HBM), in_vmem] + [pl.BlockSpec(memory_space=pltpu.SMEM)] + [in_vmem] * 3,
        out_specs=(in_vmem,) * 4,
        scratch_shapes=[
            vmem(proj_weights.shape, BF16),
            vmem((model, count), BF16),
            vmem((heads, 2, width, width), F32),
            vmem((n_ctx, heads, 2, width, width), F32),
            vmem((heads, width, width), F32),
            vmem((n_ctx, heads, width, width), F32),
            vmem((3 * model, span), F32),
            vmem((ext_rows, span), F32),
            vmem((3 * model, span), F32),
            vmem((ext_rows, span), F32),
            vmem((n_head, count, model // n_head), F32),
            vmem((n_head, count, model // n_head), F32),
            vmem((n_head, count, model // n_head), F32),
            dma((n_ctx - 1,)), dma((n_ctx - 1,)), dma((n_ctx - 1,)), dma((n_ctx - 1,)),
            dma((n_head,)), dma((n_head,)), dma((n_head,)), dma((n_head,)),
            dma((7, 2 * stages)), dma((7, 2 * stages)), dma((3,)),
        ],
        compiler_params=pltpu.CompilerParams(
            collective_id=0, has_side_effects=True, vmem_limit_bytes=44 * 1024 * 1024
        ),
        cost_estimate=pl.CostEstimate(flops=4_000_000_000, bytes_accessed=12_000_000, transcendentals=0),
    )(*(
        pltpu.with_memory_space_constraint(x, pltpu.HBM)
        for x in (
            flattened, proj_weights, init_weight, base_rates, gate_values, out_gain,
            cotangent.reshape(count, span),
        )
    ))
    anywhere = pl.BlockSpec(memory_space=pl.ANY)
    tokens_grad, proj, grad_init, grad_gain, grad_rates, gates = pl.pallas_call(
        finish_kernel,
        out_shape=(
            jax.ShapeDtypeStruct((count, model // n_head), BF16),
            jax.ShapeDtypeStruct((3 * model, span), F32),
            jax.ShapeDtypeStruct(init_weight.shape, F32),
            jax.ShapeDtypeStruct(out_gain.shape, F32),
            jax.ShapeDtypeStruct((heads,), F32),
            jax.ShapeDtypeStruct(gate_values.shape, F32),
        ),
        in_specs=[in_vmem] * 4,
        out_specs=(in_vmem, anywhere, in_vmem, in_vmem, pl.BlockSpec(memory_space=pltpu.SMEM), in_vmem),
        scratch_shapes=[dma((6,))],
        compiler_params=pltpu.CompilerParams(vmem_limit_bytes=12 * 1024 * 1024),
        cost_estimate=pl.CostEstimate(flops=0, bytes_accessed=8_000_000, transcendentals=0),
    )(*(pltpu.with_memory_space_constraint(x, pltpu.VMEM) for x in (tokens_grad, proj, ext, gates)))
    return (
        tokens_grad[None], proj.reshape(3, model, span), grad_init, grad_gain, grad_rates, gates,
    )


def solution(mesh):
    sizes = (mesh.shape["dp"], mesh.shape["ctx"], mesh.shape["head"])
    in_specs = (
        P("dp", "ctx", None),
        P(None, None, "head"),
        P("head", None, None),
        P("head"),
        P("dp", "head", "ctx"),
        P("head", None),
        P("dp", "ctx", "head"),
    )
    out_specs = (
        P("dp", "ctx", "head"),
        P(None, None, "head"),
        P("head", None, None),
        P("head", None),
        P("head"),
        P("dp", "head", "ctx"),
    )
    return jax.shard_map(
        functools.partial(body, sizes), mesh=mesh, in_specs=in_specs, out_specs=out_specs, check_vma=False
    )
```
